32 devices in a mesh: dp: 8 (over z, y), chan: 4 (over x, core).
Axes of the slice: x: 2, y: 2, z: 4, core: 2. Of those that a mesh axis runs over, the one named last changes fastest.
Arguments:
- inputs: bfloat16 [3136, 2048], P('dp', 'chan'), may hold values from -6 to 6
- conv_one: bfloat16 [9, 32, 2048], P(None, None, 'chan'), may hold values from -0.375 to 0.375
- conv_two: bfloat16 [9, 32, 2048], P(None, None, 'chan'), may hold values from -0.375 to 0.375
- probe_one: bfloat16 [2048, 512], P('chan'), may hold values from -0.125 to 0.125
- probe_two: bfloat16 [2048, 512], P('chan'), may hold values from -0.125 to 0.125
Outputs:
- restored: bfloat16 [3136, 2048], P('dp', 'chan')
- triangle: float32 [512, 512], replicated
The draws below stay inside these ranges and needn't reach their ends.
All inputs are finite; a program needn't handle non-finite values.
Results may differ from the reference program's by a relative error of at most 0.028.
Values may be sent and summed in bfloat16 or wider, within the bound.
A program may use at most 64 MiB of HBM per device.

```python
import math
import jax
import jax.numpy as jnp
from jax import lax

C = 2048
GROUP = 32
K = 512
SIDE = 7
ROWS = 3136


def shard_levels(rng, dims, cuts, low, top_value):
    loudness = 1.0
    for dim, blocks in cuts:
        steps = jax.random.uniform(jax.random.fold_in(jax.random.fold_in(rng, 6), dim), (blocks,), jnp.float32, low / len(cuts), top_value / len(cuts))
        loudness = loudness * jnp.repeat(jnp.exp(steps), dims[dim] // blocks).reshape((-1,) + (1,) * (len(dims) - 1 - dim))
    return loudness


def scatter_about(rng, dims, width, bound, cuts=(), dtype=jnp.bfloat16):
    factor_of = shard_levels(rng, dims, cuts, -0.22, 0.18) if cuts else 1.0
    drawn = jax.random.normal(rng, dims, jnp.float32) * width * factor_of
    return jnp.minimum(jnp.maximum(drawn, -bound), bound).astype(dtype)


def setup_inputs(seed: int = 0) -> dict:
    seeds = jax.random.split(jax.random.key(seed), 6)
    return {
        "inputs": scatter_about(seeds[0], (ROWS, C), 1.0, 6.0, ((0, 8), (1, 4))),
        "conv_one": scatter_about(seeds[1], (9, GROUP, C), (9 * GROUP) ** -0.5, 0.375, ((2, 4),)),
        "conv_two": scatter_about(seeds[2], (9, GROUP, C), (9 * GROUP) ** -0.5, 0.375, ((2, 4),)),
        "probe_one": scatter_about(seeds[3], (C, K), C ** -0.5, 0.125, ((0, 4),)),
        "probe_two": scatter_about(seeds[4], (C, K), C ** -0.5, 0.125, ((0, 4),)),
    }


def convolve(field, weight):
    total_rows = field.shape[0]
    group_width = weight.shape[1]
    groups = C // group_width
    images = field.reshape(total_rows // (SIDE * SIDE), SIDE, SIDE, C)
    padded = jnp.pad(images, ((0, 0), (1, 1), (1, 1), (0, 0)))
    total = jnp.zeros((total_rows, groups, group_width), jnp.float32)
    for offset in range(9):
        row_shift = offset // 3
        col_shift = offset % 3
        window = padded[:, row_shift:row_shift + SIDE, col_shift:col_shift + SIDE, :]
        window = window.reshape(total_rows, groups, group_width).astype(jnp.float32)
        kernel = weight[offset].reshape(group_width, groups, group_width).astype(jnp.float32)
        total = total + jnp.einsum('pgi,igo->pgo', window, kernel)
    return total.reshape(total_rows, C).astype(jnp.bfloat16)

def compress(responses, probe):
    sketch = jnp.dot(responses.astype(jnp.float32), probe.astype(jnp.float32), preferred_element_type=jnp.float32).astype(jnp.bfloat16)
    gram = lax.dot_general(sketch.astype(jnp.float32), sketch.astype(jnp.float32), (((0,), (0,)), ((), ())), preferred_element_type=jnp.float32)
    cross = lax.dot_general(sketch.astype(jnp.float32), responses.astype(jnp.float32), (((0,), (0,)), ((), ())), preferred_element_type=jnp.float32)
    lower = jnp.linalg.cholesky(gram)
    coeffs = lax.linalg.triangular_solve(lower, cross, left_side=True, lower=True).astype(jnp.bfloat16)
    mapped = lax.linalg.triangular_solve(lower, coeffs.astype(jnp.float32), left_side=True, lower=True, transpose_a=True).astype(jnp.bfloat16)
    return (jnp.dot(sketch.astype(jnp.float32), mapped.astype(jnp.float32), preferred_element_type=jnp.float32).astype(jnp.bfloat16), lower)

def reference(inputs, conv_one, conv_two, probe_one, probe_two):
    responses_one = convolve(inputs, conv_one)
    restored_one, lower_one = compress(responses_one, probe_one)
    activated = jnp.maximum(restored_one, jnp.zeros((), jnp.bfloat16))
    responses_two = convolve(activated, conv_two)
    restored, lower_two = compress(responses_two, probe_two)
    triangle = jnp.transpose(lower_two) * (1.0 / math.sqrt(ROWS))
    return (restored, triangle)
```

```python
import functools
import math

import jax
import jax.numpy as jnp
from jax import lax
from jax.experimental import pallas as pl
from jax.experimental.pallas import tpu as pltpu
from jax.sharding import PartitionSpec as P

SIDE = 7
PAD = 16
BLOCK = 128
PANEL = 16
F32 = jnp.float32
BF16 = jnp.bfloat16
VMEM_LIMIT = 48 * 1024 * 1024


def dot_f32(a, b, dims):
    return lax.dot_general(
        a, b, (dims, ((), ())), preferred_element_type=F32, precision=lax.Precision.HIGHEST
    )


def dot_bf16(a, b, dims):
    return lax.dot_general(a, b, (dims, ((), ())), preferred_element_type=F32)


def conv_into(field_ref, weight_ref, pad_ref, out_ref):
    rows, width = field_ref.shape
    group = weight_ref.shape[1]
    lanes = min(256, width)
    pad_ref[0:PAD, :] = jnp.zeros((PAD, width), F32)
    pad_ref[PAD + rows : PAD + rows + PAD, :] = jnp.zeros((PAD, width), F32)
    pad_ref[PAD : PAD + rows, :] = field_ref[...].astype(F32)
    place = lax.broadcasted_iota(jnp.int32, (rows, lanes), 0).astype(F32)
    pixel = place - (SIDE * SIDE) * jnp.floor((place + 0.5) * (1.0 / (SIDE * SIDE)))
    line = jnp.floor((pixel + 0.5) * (1.0 / SIDE))
    column = pixel - SIDE * line
    one, zero = jnp.ones((), F32), jnp.zeros((), F32)
    line_ok = (jnp.where(line > 0.5, one, zero), None, jnp.where(line < SIDE - 1.5, one, zero))
    column_ok = (jnp.where(column > 0.5, one, zero), None, jnp.where(column < SIDE - 1.5, one, zero))
    same = (
        lax.broadcasted_iota(jnp.int32, (lanes, lanes), 0) // group
        == lax.broadcasted_iota(jnp.int32, (lanes, lanes), 1) // group
    )
    for start in range(0, width, lanes):
        total = None
        for a in range(3):
            for b in range(3):
                shift = (a - 1) * SIDE + (b - 1)
                window = pad_ref[PAD + shift : PAD + shift + rows, start : start + lanes]
                if line_ok[a] is not None:
                    window = window * line_ok[a]
                if column_ok[b] is not None:
                    window = window * column_ok[b]
                small = weight_ref[3 * a + b, :, start : start + lanes]
                full = jnp.concatenate([small] * (lanes // group), axis=0)
                full = jnp.where(same, full, jnp.zeros((), BF16))
                part = dot_bf16(window.astype(BF16), full, ((1,), (0,)))
                total = part if total is None else total + part
        out_ref[:, start : start + lanes] = total.astype(BF16)


def split3(x):
    high = x.astype(BF16)
    rest = x - high.astype(F32)
    middle = rest.astype(BF16)
    low = (rest - middle.astype(F32)).astype(BF16)
    return high, middle, low


def eliminate_block(work_ref):
    row_of = lax.broadcasted_iota(jnp.int32, (PANEL, BLOCK), 0)
    for panel in range(BLOCK // PANEL):
        top = panel * PANEL
        left = work_ref[top : top + PANEL, 0:BLOCK]
        right = work_ref[top : top + PANEL, BLOCK : 2 * BLOCK]
        cols = [
            jnp.broadcast_to(left[:, top + k : top + k + 1], (PANEL, BLOCK)) for k in range(PANEL)
        ]
        scale = jnp.zeros((PANEL, BLOCK), F32)
        for i in range(PANEL):
            pivot = jnp.broadcast_to(cols[i][i : i + 1, :], (PANEL, BLOCK))
            root = lax.rsqrt(pivot)
            root = root * (1.5 - 0.5 * pivot * root * root)
            scale = jnp.where(row_of == i, root, scale)
            if i < PANEL - 1:
                factor = jnp.where(row_of > i, cols[i] * (root * root), 0.0)
                for k in range(i + 1, PANEL):
                    cols[k] = cols[k] - factor * cols[k][i : i + 1, :]
                left = left - factor * left[i : i + 1, :]
                right = right - factor * right[i : i + 1, :]
        left = left * scale
        right = right * scale
        lane_of = lax.broadcasted_iota(jnp.int32, (PANEL, BLOCK), 1)
        left = jnp.where(lane_of >= top + row_of, left, 0.0)
        work_ref[top : top + PANEL, 0:BLOCK] = left
        work_ref[top : top + PANEL, BLOCK : 2 * BLOCK] = right
        if top + PANEL < BLOCK:
            rest = top + PANEL
            h, m, l = split3(left)
            hr, mr, lr = split3(right)
            first = jnp.concatenate([h, h, m, h, l, m], axis=0)
            second = jnp.concatenate(
                [
                    jnp.concatenate([h, m, h, l, h, m], axis=0),
                    jnp.concatenate([hr, mr, hr, lr, hr, mr], axis=0),
                ],
                axis=1,
            )
            update = dot_bf16(first, second, ((0,), (0,)))
            work_ref[rest:BLOCK, :] = work_ref[rest:BLOCK, :] - update[rest:BLOCK, :]


def eliminate(big_ref, work_ref, size):
    blocks = size // BLOCK
    square = (BLOCK, BLOCK)
    eye = jnp.where(
        lax.broadcasted_iota(jnp.int32, square, 0) == lax.broadcasted_iota(jnp.int32, square, 1),
        1.0,
        0.0,
    )

    @pl.loop(0, blocks)
    def _(b):
        at = pl.ds(pl.multiple_of(b * BLOCK, BLOCK), BLOCK)
        work_ref[:, 0:BLOCK] = big_ref[at, at]
        work_ref[:, BLOCK : 2 * BLOCK] = eye
        eliminate_block(work_ref)
        inverse = work_ref[:, BLOCK : 2 * BLOCK]
        big_ref[at, :] = dot_f32(inverse, big_ref[at, :], ((1,), (0,)))
        big_ref[at, at] = work_ref[:, 0:BLOCK]

        @pl.loop(b + 1, blocks)
        def _(other):
            to = pl.ds(pl.multiple_of(other * BLOCK, BLOCK), BLOCK)
            big_ref[to, :] = big_ref[to, :] - dot_f32(big_ref[at, to], big_ref[at, :], ((0,), (0,)))


def solve_into(gram_ref, cross_ref, mapped_ref, upper_ref, big_ref, work_ref):
    size = gram_ref.shape[0]
    square = (size, size)
    row_of = lax.broadcasted_iota(jnp.int32, square, 0)
    lane_of = lax.broadcasted_iota(jnp.int32, square, 1)
    big_ref[:, 0:size] = gram_ref[...]
    big_ref[:, size : 2 * size] = jnp.where(row_of == lane_of, 1.0, 0.0)
    eliminate(big_ref, work_ref, size)
    if upper_ref is not None:
        upper_ref[...] = jnp.where(lane_of >= row_of, big_ref[:, 0:size], 0.0)
    inverse = big_ref[:, size : 2 * size]
    coeffs = dot_f32(cross_ref[...], inverse, ((1,), (1,))).astype(BF16)
    mapped_ref[...] = dot_f32(coeffs.astype(F32), inverse, ((1,), (0,))).astype(BF16)


def conv_kernel(field_ref, weight_ref, probe_ref, responses_ref, partial_ref, pad_ref):
    conv_into(field_ref, weight_ref, pad_ref, responses_ref)
    partial_ref[...] = dot_bf16(responses_ref[...], probe_ref[...], ((1,), (0,)))


def conv_call(field, weight, probe):
    rows, width = field.shape
    return pl.pallas_call(
        conv_kernel,
        out_shape=(
            jax.ShapeDtypeStruct((rows, width), BF16),
            jax.ShapeDtypeStruct((rows, probe.shape[1]), F32),
        ),
        scratch_shapes=[pltpu.VMEM((rows + 2 * PAD, width), F32)],
        compiler_params=pltpu.CompilerParams(vmem_limit_bytes=VMEM_LIMIT),
    )(field, weight, probe)


def solve_call(gram, cross):
    size = gram.shape[0]
    return pl.pallas_call(
        solve_into,
        out_shape=(
            jax.ShapeDtypeStruct(cross.shape, BF16),
            jax.ShapeDtypeStruct(gram.shape, F32),
        ),
        scratch_shapes=[pltpu.VMEM((size, 2 * size), F32), pltpu.VMEM((BLOCK, 2 * BLOCK), F32)],
        compiler_params=pltpu.CompilerParams(vmem_limit_bytes=VMEM_LIMIT),
    )(gram, cross)


def layer(field, weight, probe):
    responses, partial = conv_call(field, weight, probe)
    sketch = lax.psum(partial, "chan").astype(BF16)
    gram = dot_bf16(sketch, sketch, ((0,), (0,)))
    cross = dot_bf16(responses, sketch, ((0,), (0,)))
    gram = lax.psum(gram, "dp")
    cross = lax.psum_scatter(cross, "dp", scatter_dimension=0, tiled=True)
    mapped, upper = solve_call(gram, cross)
    mapped = lax.all_gather(mapped, "dp", axis=0, tiled=True)
    return dot_bf16(sketch, mapped, ((1,), (1,))).astype(BF16), upper


def per_device(inputs, conv_one, conv_two, probe_one, probe_two):
    restored_one, _ = layer(inputs, conv_one, probe_one)
    activated = jnp.maximum(restored_one, jnp.zeros((), BF16))
    restored, upper = layer(activated, conv_two, probe_two)
    total_rows = inputs.shape[0] * lax.axis_size("dp")
    return (restored, upper * (1.0 / math.sqrt(total_rows)))


def solution(mesh):
    in_specs = (
        P("dp", "chan"),
        P(None, None, "chan"),
        P(None, None, "chan"),
        P("chan", None),
        P("chan", None),
    )
    return jax.shard_map(
        per_device, mesh=mesh, in_specs=in_specs, out_specs=(P("dp", "chan"), P()), check_vma=False
    )
```

```python
import functools
import math

import jax
import jax.numpy as jnp
from jax import lax
from jax.experimental import pallas as pl
from jax.experimental.pallas import tpu as pltpu
from jax.sharding import PartitionSpec as P

SIDE = 7
PAD = 16
BLOCK = 128
PANEL = 16
F32 = jnp.float32
BF16 = jnp.bfloat16
VMEM_LIMIT = 48 * 1024 * 1024


def dot_f32(a, b, dims):
    return lax.dot_general(
        a, b, (dims, ((), ())), preferred_element_type=F32, precision=lax.Precision.HIGHEST
    )


def dot_bf16(a, b, dims):
    return lax.dot_general(a, b, (dims, ((), ())), preferred_element_type=F32)


def conv_into(field_ref, weight_ref, pad_ref, out_ref):
    rows, width = field_ref.shape
    group = weight_ref.shape[1]
    lanes = min(256, width)
    pad_ref[0:PAD, :] = jnp.zeros((PAD, width), F32)
    pad_ref[PAD + rows : PAD + rows + PAD, :] = jnp.zeros((PAD, width), F32)
    pad_ref[PAD : PAD + rows, :] = field_ref[...].astype(F32)
    place = lax.broadcasted_iota(jnp.int32, (rows, lanes), 0).astype(F32)
    pixel = place - (SIDE * SIDE) * jnp.floor((place + 0.5) * (1.0 / (SIDE * SIDE)))
    line = jnp.floor((pixel + 0.5) * (1.0 / SIDE))
    column = pixel - SIDE * line
    one, zero = jnp.ones((), F32), jnp.zeros((), F32)
    line_ok = (jnp.where(line > 0.5, one, zero), None, jnp.where(line < SIDE - 1.5, one, zero))
    column_ok = (jnp.where(column > 0.5, one, zero), None, jnp.where(column < SIDE - 1.5, one, zero))
    same = (
        lax.broadcasted_iota(jnp.int32, (lanes, lanes), 0) // group
        == lax.broadcasted_iota(jnp.int32, (lanes, lanes), 1) // group
    )
    for start in range(0, width, lanes):
        total = None
        for a in range(3):
            for b in range(3):
                shift = (a - 1) * SIDE + (b - 1)
                window = pad_ref[PAD + shift : PAD + shift + rows, start : start + lanes]
                if line_ok[a] is not None:
                    window = window * line_ok[a]
                if column_ok[b] is not None:
                    window = window * column_ok[b]
                small = weight_ref[3 * a + b, :, start : start + lanes]
                full = jnp.concatenate([small] * (lanes // group), axis=0)
                full = jnp.where(same, full, jnp.zeros((), BF16))
                part = dot_bf16(window.astype(BF16), full, ((1,), (0,)))
                total = part if total is None else total + part
        out_ref[0:rows, start : start + lanes] = total.astype(BF16)
    if out_ref.shape[0] > rows:
        out_ref[rows:, :] = jnp.zeros((out_ref.shape[0] - rows, width), BF16)


def split3(x):
    high = x.astype(BF16)
    rest = x - high.astype(F32)
    middle = rest.astype(BF16)
    low = (rest - middle.astype(F32)).astype(BF16)
    return high, middle, low


def eliminate_block(work_ref):
    row_of = lax.broadcasted_iota(jnp.int32, (PANEL, BLOCK), 0)
    for panel in range(BLOCK // PANEL):
        top = panel * PANEL
        left = work_ref[top : top + PANEL, 0:BLOCK]
        right = work_ref[top : top + PANEL, BLOCK : 2 * BLOCK]
        cols = [
            jnp.broadcast_to(left[:, top + k : top + k + 1], (PANEL, BLOCK)) for k in range(PANEL)
        ]
        scale = jnp.zeros((PANEL, BLOCK), F32)
        for i in range(PANEL):
            pivot = jnp.broadcast_to(cols[i][i : i + 1, :], (PANEL, BLOCK))
            root = lax.rsqrt(pivot)
            root = root * (1.5 - 0.5 * pivot * root * root)
            scale = jnp.where(row_of == i, root, scale)
            if i < PANEL - 1:
                factor = jnp.where(row_of > i, cols[i] * (root * root), 0.0)
                for k in range(i + 1, PANEL):
                    cols[k] = cols[k] - factor * cols[k][i : i + 1, :]
                left = left - factor * left[i : i + 1, :]
                right = right - factor * right[i : i + 1, :]
        left = left * scale
        right = right * scale
        lane_of = lax.broadcasted_iota(jnp.int32, (PANEL, BLOCK), 1)
        left = jnp.where(lane_of >= top + row_of, left, 0.0)
        work_ref[top : top + PANEL, 0:BLOCK] = left
        work_ref[top : top + PANEL, BLOCK : 2 * BLOCK] = right
        if top + PANEL < BLOCK:
            rest = top + PANEL
            h, m, l = split3(left)
            hr, mr, lr = split3(right)
            first = jnp.concatenate([h, h, m, h, l, m], axis=0)
            second = jnp.concatenate(
                [
                    jnp.concatenate([h, m, h, l, h, m], axis=0),
                    jnp.concatenate([hr, mr, hr, lr, hr, mr], axis=0),
                ],
                axis=1,
            )
            update = dot_bf16(first, second, ((0,), (0,)))
            work_ref[rest:BLOCK, :] = work_ref[rest:BLOCK, :] - update[rest:BLOCK, :]


def eliminate(big_ref, work_ref, size):
    blocks = size // BLOCK
    square = (BLOCK, BLOCK)
    eye = jnp.where(
        lax.broadcasted_iota(jnp.int32, square, 0) == lax.broadcasted_iota(jnp.int32, square, 1),
        1.0,
        0.0,
    )

    @pl.loop(0, blocks)
    def _(b):
        at = pl.ds(pl.multiple_of(b * BLOCK, BLOCK), BLOCK)
        work_ref[:, 0:BLOCK] = big_ref[at, at]
        work_ref[:, BLOCK : 2 * BLOCK] = eye
        eliminate_block(work_ref)
        inverse = work_ref[:, BLOCK : 2 * BLOCK]
        big_ref[at, :] = dot_f32(inverse, big_ref[at, :], ((1,), (0,)))
        big_ref[at, at] = work_ref[:, 0:BLOCK]

        @pl.loop(b + 1, blocks)
        def _(other):
            to = pl.ds(pl.multiple_of(other * BLOCK, BLOCK), BLOCK)
            big_ref[to, :] = big_ref[to, :] - dot_f32(big_ref[at, to], big_ref[at, :], ((0,), (0,)))


def identity_into(big_ref, size):
    square = (size, size)
    row_of = lax.broadcasted_iota(jnp.int32, square, 0)
    lane_of = lax.broadcasted_iota(jnp.int32, square, 1)
    big_ref[:, size : 2 * size] = jnp.where(row_of == lane_of, 1.0, 0.0)


def exchange(axis, me, count, source, target, send_sem, recv_sem):
    copies = []
    for j in range(1, count):
        peer = lax.rem(me + j, count)
        copy = pltpu.make_async_remote_copy(
            src_ref=source(j, peer),
            dst_ref=target(j, peer),
            send_sem=send_sem.at[j],
            recv_sem=recv_sem.at[j],
            device_id={axis: peer},
            device_id_type=pl.DeviceIdType.MESH,
        )
        copy.start()
        copies.append(copy)
    return copies


def arrived(axis, me, count, target, send_sem, recv_sem):
    for j in range(1, count):
        sender = lax.rem(me + count - j, count)
        pltpu.make_async_remote_copy(
            src_ref=target(j, sender),
            dst_ref=target(j, sender),
            send_sem=send_sem.at[j],
            recv_sem=recv_sem.at[j],
            device_id={axis: sender},
            device_id_type=pl.DeviceIdType.MESH,
        ).wait_recv()


def layer_kernel(
    nd, nc, last, total_rows,
    field_ref, weight_ref, probe_ref, out_ref, upper_ref,
    pad_ref, resp_ref, part_ref, part_in_ref, sketch_ref, gpart_ref, gin_ref, gsum_ref,
    cpart_ref, cin_ref, map_ref, big_ref, work_ref,
    s_part, r_part, s_sketch, r_sketch, s_gram, r_gram, s_rows, r_rows, s_blocks, r_blocks,
    s_cross, r_cross, s_map, r_map,
):
    d = lax.axis_index("dp")
    c = lax.axis_index("chan")
    rows, width = field_ref.shape
    size = probe_ref.shape[1]
    padded = resp_ref.shape[0]
    share = size // nc
    gram_rows = share // nd
    cross_rows = width // nd

    barrier = pltpu.get_barrier_semaphore()
    for j in range(1, nd):
        pl.semaphore_signal(
            barrier, inc=1, device_id={"dp": lax.rem(d + j, nd)}, device_id_type=pl.DeviceIdType.MESH
        )
    for j in range(1, nc):
        pl.semaphore_signal(
            barrier, inc=1, device_id={"chan": lax.rem(c + j, nc)}, device_id_type=pl.DeviceIdType.MESH
        )

    conv_into(field_ref, weight_ref, pad_ref, resp_ref)
    responses = resp_ref[...]
    for j in range(nc):
        block = dot_bf16(responses, probe_ref[:, j * share : (j + 1) * share], ((1,), (0,)))
        part_ref[j] = block.astype(BF16)
    pl.semaphore_wait(barrier, nd + nc - 2)

    started = exchange(
        "chan", c, nc, lambda j, p: part_ref.at[p], lambda j, p: part_in_ref.at[j], s_part, r_part
    )
    identity_into(big_ref, size)
    arrived("chan", c, nc, lambda j, p: part_in_ref.at[j], s_part, r_part)
    mine = part_ref[c].astype(F32)
    for j in range(1, nc):
        mine = mine + part_in_ref[j].astype(F32)
    mine = mine.astype(BF16)
    sketch_ref[c] = mine
    started += exchange(
        "chan", c, nc, lambda j, p: sketch_ref.at[c], lambda j, p: sketch_ref.at[c], s_sketch, r_sketch
    )
    arrived("chan", c, nc, lambda j, p: sketch_ref.at[p], s_sketch, r_sketch)
    sketch = jnp.concatenate([sketch_ref[j] for j in range(nc)], axis=1)

    gram = dot_bf16(mine, sketch, ((0,), (0,)))
    for j in range(nd):
        gpart_ref[j] = gram[j * gram_rows : (j + 1) * gram_rows, :]
    started += exchange(
        "dp", d, nd, lambda j, p: gpart_ref.at[p], lambda j, p: gin_ref.at[j], s_gram, r_gram
    )
    cross = dot_bf16(responses, sketch, ((0,), (0,)))
    for j in range(nd):
        cpart_ref[j] = cross[j * cross_rows : (j + 1) * cross_rows, :]
    arrived("dp", d, nd, lambda j, p: gin_ref.at[j], s_gram, r_gram)
    total = gpart_ref[d]
    for j in range(1, nd):
        total = total + gin_ref[j]
    gsum_ref[c, d] = total
    started += exchange(
        "dp", d, nd, lambda j, p: gsum_ref.at[c, d], lambda j, p: gsum_ref.at[c, d], s_rows, r_rows
    )
    arrived("dp", d, nd, lambda j, p: gsum_ref.at[c, p], s_rows, r_rows)
    started += exchange(
        "chan", c, nc, lambda j, p: gsum_ref.at[c], lambda j, p: gsum_ref.at[c], s_blocks, r_blocks
    )
    arrived("chan", c, nc, lambda j, p: gsum_ref.at[p], s_blocks, r_blocks)
    started += exchange(
        "dp", d, nd, lambda j, p: cpart_ref.at[p], lambda j, p: cin_ref.at[j], s_cross, r_cross
    )
    for k in range(nc):
        for j in range(nd):
            top = k * share + j * gram_rows
            big_ref[top : top + gram_rows, 0:size] = gsum_ref[k, j]

    eliminate(big_ref, work_ref, size)
    if last:
        square = (size, size)
        keep = lax.broadcasted_iota(jnp.int32, square, 1) >= lax.broadcasted_iota(jnp.int32, square, 0)
        upper_ref[...] = jnp.where(keep, big_ref[:, 0:size], 0.0) * (1.0 / math.sqrt(total_rows))

    arrived("dp", d, nd, lambda j, p: cin_ref.at[j], s_cross, r_cross)
    own = cpart_ref[d]
    for j in range(1, nd):
        own = own + cin_ref[j]
    inverse = big_ref[:, size : 2 * size]
    coeffs = dot_f32(own, inverse, ((1,), (1,))).astype(BF16)
    map_ref[d] = dot_f32(coeffs.astype(F32), inverse, ((1,), (0,))).astype(BF16)
    started += exchange(
        "dp", d, nd, lambda j, p: map_ref.at[d], lambda j, p: map_ref.at[d], s_map, r_map
    )
    arrived("dp", d, nd, lambda j, p: map_ref.at[p], s_map, r_map)
    if cross_rows % 16 == 0:
        mapped = jnp.concatenate([map_ref[j] for j in range(nd)], axis=0)
    else:
        mapped = jnp.concatenate([map_ref[j].astype(F32) for j in range(nd)], axis=0).astype(BF16)
    restored = dot_bf16(sketch, mapped, ((1,), (1,)))
    if not last:
        restored = jnp.maximum(restored, 0.0)
    out_ref[...] = restored[0:rows, :].astype(BF16)
    for copy in started:
        copy.wait_send()


def first_kernel(nd, nc, total_rows, field_ref, weight_ref, probe_ref, out_ref, *rest):
    layer_kernel(nd, nc, False, total_rows, field_ref, weight_ref, probe_ref, out_ref, None, *rest)


def last_kernel(nd, nc, total_rows, *refs):
    layer_kernel(nd, nc, True, total_rows, *refs)


def layer(field, weight, probe, last):
    nd, nc = lax.axis_size("dp"), lax.axis_size("chan")
    rows, width = field.shape
    size = probe.shape[1]
    padded = -(-rows // 16) * 16
    share = size // nc
    gram_rows = share // nd
    cross_rows = width // nd
    restored = jax.ShapeDtypeStruct((rows, width), BF16)
    upper = jax.ShapeDtypeStruct((size, size), F32)
    chan_sems = pltpu.SemaphoreType.DMA((nc,))
    dp_sems = pltpu.SemaphoreType.DMA((nd,))
    return pl.pallas_call(
        functools.partial(last_kernel if last else first_kernel, nd, nc, rows * nd),
        out_shape=(restored, upper) if last else restored,
        scratch_shapes=[
            pltpu.VMEM((rows + 2 * PAD, width), F32),
            pltpu.VMEM((padded, width), BF16),
            pltpu.VMEM((nc, padded, share), BF16),
            pltpu.VMEM((nc, padded, share), BF16),
            pltpu.VMEM((nc, padded, share), BF16),
            pltpu.VMEM((nd, gram_rows, size), F32),
            pltpu.VMEM((nd, gram_rows, size), F32),
            pltpu.VMEM((nc, nd, gram_rows, size), F32),
            pltpu.VMEM((nd, cross_rows, size), F32),
            pltpu.VMEM((nd, cross_rows, size), F32),
            pltpu.VMEM((nd, cross_rows, size), BF16),
            pltpu.VMEM((size, 2 * size), F32),
            pltpu.VMEM((BLOCK, 2 * BLOCK), F32),
        ]
        + [chan_sems] * 4
        + [dp_sems] * 4
        + [chan_sems] * 2
        + [dp_sems] * 4,
        compiler_params=pltpu.CompilerParams(
            vmem_limit_bytes=VMEM_LIMIT, collective_id=1 if last else 0, has_side_effects=True
        ),
    )(field, weight, probe)


def per_device(inputs, conv_one, conv_two, probe_one, probe_two):
    activated = layer(inputs, conv_one, probe_one, False)
    return layer(activated, conv_two, probe_two, True)


def solution(mesh):
    in_specs = (
        P("dp", "chan"),
        P(None, None, "chan"),
        P(None, None, "chan"),
        P("chan", None),
        P("chan", None),
    )
    return jax.shard_map(
        per_device, mesh=mesh, in_specs=in_specs, out_specs=(P("dp", "chan"), P()), check_vma=False
    )
```

```python
import functools
import math

import jax
import jax.numpy as jnp
from jax import lax
from jax.experimental import pallas as pl
from jax.experimental.pallas import tpu as pltpu
from jax.sharding import PartitionSpec as P

SIDE = 7
PAD = 16
BLOCK = 128
PANEL = 16
F32 = jnp.float32
BF16 = jnp.bfloat16
VMEM_LIMIT = 48 * 1024 * 1024


def dot_f32(a, b, dims):
    return lax.dot_general(
        a, b, (dims, ((), ())), preferred_element_type=F32, precision=lax.Precision.HIGHEST
    )


def dot_bf16(a, b, dims):
    return lax.dot_general(a, b, (dims, ((), ())), preferred_element_type=F32)


def conv_into(field_ref, weight_ref, pad_ref, out_ref):
    rows, width = field_ref.shape
    group = weight_ref.shape[1]
    lanes = min(256, width)
    pad_ref[0:PAD, :] = jnp.zeros((PAD, width), F32)
    pad_ref[PAD + rows : PAD + rows + PAD, :] = jnp.zeros((PAD, width), F32)
    pad_ref[PAD : PAD + rows, :] = field_ref[...].astype(F32)
    place = lax.broadcasted_iota(jnp.int32, (rows, lanes), 0).astype(F32)
    pixel = place - (SIDE * SIDE) * jnp.floor((place + 0.5) * (1.0 / (SIDE * SIDE)))
    line = jnp.floor((pixel + 0.5) * (1.0 / SIDE))
    column = pixel - SIDE * line
    one, zero = jnp.ones((), F32), jnp.zeros((), F32)
    line_ok = (jnp.where(line > 0.5, one, zero), None, jnp.where(line < SIDE - 1.5, one, zero))
    column_ok = (jnp.where(column > 0.5, one, zero), None, jnp.where(column < SIDE - 1.5, one, zero))
    same = (
        lax.broadcasted_iota(jnp.int32, (lanes, lanes), 0) // group
        == lax.broadcasted_iota(jnp.int32, (lanes, lanes), 1) // group
    )
    for start in range(0, width, lanes):
        total = None
        for a in range(3):
            for b in range(3):
                shift = (a - 1) * SIDE + (b - 1)
                window = pad_ref[PAD + shift : PAD + shift + rows, start : start + lanes]
                if line_ok[a] is not None:
                    window = window * line_ok[a]
                if column_ok[b] is not None:
                    window = window * column_ok[b]
                small = weight_ref[3 * a + b, :, start : start + lanes]
                full = jnp.concatenate([small] * (lanes // group), axis=0)
                full = jnp.where(same, full, jnp.zeros((), BF16))
                part = dot_bf16(window.astype(BF16), full, ((1,), (0,)))
                total = part if total is None else total + part
        out_ref[0:rows, start : start + lanes] = total.astype(BF16)
    if out_ref.shape[0] > rows:
        out_ref[rows:, :] = jnp.zeros((out_ref.shape[0] - rows, width), BF16)


def split3(x):
    high = x.astype(BF16)
    rest = x - high.astype(F32)
    middle = rest.astype(BF16)
    low = (rest - middle.astype(F32)).astype(BF16)
    return high, middle, low


def stack_first(x, axis):
    h, m, l = split3(x)
    return jnp.concatenate([h, h, m, h, l, m], axis=axis)


def stack_second(x):
    h, m, l = split3(x)
    return jnp.concatenate([h, m, h, l, h, m], axis=0)


def eliminate_block(work_ref):
    row_of = lax.broadcasted_iota(jnp.int32, (PANEL, BLOCK), 0)
    for panel in range(BLOCK // PANEL):
        top = panel * PANEL
        left = work_ref[top : top + PANEL, 0:BLOCK]
        right = work_ref[top : top + PANEL, BLOCK : 2 * BLOCK]
        cols = [
            jnp.broadcast_to(left[:, top + k : top + k + 1], (PANEL, BLOCK)) for k in range(PANEL)
        ]
        scale = jnp.zeros((PANEL, BLOCK), F32)
        for i in range(PANEL):
            pivot = jnp.broadcast_to(cols[i][i : i + 1, :], (PANEL, BLOCK))
            root = lax.rsqrt(pivot)
            root = root * (1.5 - 0.5 * pivot * root * root)
            scale = jnp.where(row_of == i, root, scale)
            if i < PANEL - 1:
                factor = jnp.where(row_of > i, cols[i] * (root * root), 0.0)
                for k in range(i + 1, PANEL):
                    cols[k] = cols[k] - factor * cols[k][i : i + 1, :]
                left = left - factor * left[i : i + 1, :]
                right = right - factor * right[i : i + 1, :]
        left = left * scale
        right = right * scale
        lane_of = lax.broadcasted_iota(jnp.int32, (PANEL, BLOCK), 1)
        left = jnp.where(lane_of >= top + row_of, left, 0.0)
        work_ref[top : top + PANEL, 0:BLOCK] = left
        work_ref[top : top + PANEL, BLOCK : 2 * BLOCK] = right
        if top + PANEL < BLOCK:
            rest = top + PANEL
            second = jnp.concatenate([stack_second(left), stack_second(right)], axis=1)
            update = dot_bf16(stack_first(left, 0), second, ((0,), (0,)))
            work_ref[rest:BLOCK, :] = work_ref[rest:BLOCK, :] - update[rest:BLOCK, :]


def eliminate(big_ref, work_ref, stack_ref, diag_ref, size, between):
    blocks = size // BLOCK
    square = (BLOCK, BLOCK)
    eye = jnp.where(
        lax.broadcasted_iota(jnp.int32, square, 0) == lax.broadcasted_iota(jnp.int32, square, 1),
        1.0,
        0.0,
    )

    @pl.loop(0, blocks)
    def _(b):
        pl.when(b == 1)(between)
        at = pl.ds(pl.multiple_of(b * BLOCK, BLOCK), BLOCK)
        work_ref[:, 0:BLOCK] = big_ref[at, at]
        work_ref[:, BLOCK : 2 * BLOCK] = eye
        eliminate_block(work_ref)
        diag_ref[b] = work_ref[:, 0:BLOCK]
        inverse = work_ref[:, BLOCK : 2 * BLOCK]
        big_ref[at, at] = eye
        row = dot_bf16(stack_first(inverse, 1), stack_second(big_ref[at, :]), ((1,), (0,)))
        big_ref[at, :] = row
        stack_ref[...] = stack_second(row)

        @pl.loop(b + 1, blocks)
        def _(other):
            to = pl.ds(pl.multiple_of(other * BLOCK, BLOCK), BLOCK)
            big_ref[to, at] = jnp.zeros(square, F32)
            factor = stack_first(big_ref[at, to], 0)
            big_ref[to, :] = big_ref[to, :] - dot_bf16(factor, stack_ref[...], ((0,), (0,)))


def exchange(axis, me, count, source, target, send_sem, recv_sem):
    copies = []
    for j in range(1, count):
        peer = lax.rem(me + j, count)
        copy = pltpu.make_async_remote_copy(
            src_ref=source(j, peer),
            dst_ref=target(j, peer),
            send_sem=send_sem.at[j],
            recv_sem=recv_sem.at[j],
            device_id={axis: peer},
            device_id_type=pl.DeviceIdType.MESH,
        )
        copy.start()
        copies.append(copy)
    return copies


def arrived(axis, me, count, target, send_sem, recv_sem):
    for j in range(1, count):
        sender = lax.rem(me + count - j, count)
        pltpu.make_async_remote_copy(
            src_ref=target(j, sender),
            dst_ref=target(j, sender),
            send_sem=send_sem.at[j],
            recv_sem=recv_sem.at[j],
            device_id={axis: sender},
            device_id_type=pl.DeviceIdType.MESH,
        ).wait_recv()


def send(axis, peer, source, target, send_sem, recv_sem):
    copy = pltpu.make_async_remote_copy(
        src_ref=source,
        dst_ref=target,
        send_sem=send_sem,
        recv_sem=recv_sem,
        device_id={axis: peer},
        device_id_type=pl.DeviceIdType.MESH,
    )
    copy.start()
    return copy


def expect(axis, sender, target, send_sem, recv_sem):
    pltpu.make_async_remote_copy(
        src_ref=target,
        dst_ref=target,
        send_sem=send_sem,
        recv_sem=recv_sem,
        device_id={axis: sender},
        device_id_type=pl.DeviceIdType.MESH,
    ).wait_recv()


def gather(axis, me, count, slot, far_send, far_recv, mate_send, mate_recv):
    high, low = me // 2, me % 2
    mate = me + 1 - 2 * low
    pairs = count // 2
    copies = [
        send(axis, 2 * lax.rem(high + j, pairs) + low, slot(me), slot(me), far_send.at[j], far_recv.at[j])
        for j in range(1, pairs)
    ]
    copies.append(send(axis, mate, slot(me), slot(me), mate_send.at[0], mate_recv.at[0]))
    for j in range(1, pairs):
        sender = 2 * lax.rem(high + pairs - j, pairs) + low
        expect(axis, sender, slot(sender), far_send.at[j], far_recv.at[j])
        copies.append(send(axis, mate, slot(sender), slot(sender), mate_send.at[j], mate_recv.at[j]))
    expect(axis, mate, slot(mate), mate_send.at[0], mate_recv.at[0])
    for j in range(1, pairs):
        origin = 2 * lax.rem(high + pairs - j, pairs) + 1 - low
        expect(axis, mate, slot(origin), mate_send.at[j], mate_recv.at[j])
    return copies


def layer_kernel(
    nd, nc, last, total_rows,
    field_ref, weight_ref, probe_ref, out_ref, upper_ref,
    pad_ref, resp_ref, part_ref, part_in_ref, sketch_ref, gpart_ref, gin_ref, gsum_ref,
    cpart_ref, cmate_ref, cin_ref, map_ref, big_ref, work_ref, stack_ref, diag_ref,
    s_part, r_part, s_sketch, r_sketch, s_sketch2, r_sketch2, s_blocks, r_blocks, s_blocks2, r_blocks2,
    s_gram, r_gram, s_rows, r_rows, s_rows2, r_rows2, s_mate, r_mate, s_cross, r_cross,
    s_map, r_map, s_map2, r_map2,
):
    d = lax.axis_index("dp")
    c = lax.axis_index("chan")
    rows, width = field_ref.shape
    size = probe_ref.shape[1]
    padded = resp_ref.shape[0]
    share = size // nc
    gram_rows = share // nd
    cross_rows = width // nd

    barrier = pltpu.get_barrier_semaphore()
    for j in range(1, nd):
        pl.semaphore_signal(
            barrier, inc=1, device_id={"dp": lax.rem(d + j, nd)}, device_id_type=pl.DeviceIdType.MESH
        )
    for j in range(1, nc):
        pl.semaphore_signal(
            barrier, inc=1, device_id={"chan": lax.rem(c + j, nc)}, device_id_type=pl.DeviceIdType.MESH
        )

    conv_into(field_ref, weight_ref, pad_ref, resp_ref)
    responses = resp_ref[...]
    for j in range(nc):
        block = dot_bf16(responses, probe_ref[:, j * share : (j + 1) * share], ((1,), (0,)))
        part_ref[j] = block.astype(BF16)
    pl.semaphore_wait(barrier, nd + nc - 2)

    started = exchange(
        "chan", c, nc, lambda j, p: part_ref.at[p], lambda j, p: part_in_ref.at[j], s_part, r_part
    )
    big_ref[...] = jnp.zeros((size, size), F32)
    arrived("chan", c, nc, lambda j, p: part_in_ref.at[j], s_part, r_part)
    mine = part_ref[c].astype(F32)
    for j in range(1, nc):
        mine = mine + part_in_ref[j].astype(F32)
    mine = mine.astype(BF16)
    sketch_ref[c] = mine
    started += gather(
        "chan", c, nc, lambda i: sketch_ref.at[i], s_sketch, r_sketch, s_sketch2, r_sketch2
    )
    sketch = jnp.concatenate([sketch_ref[j] for j in range(nc)], axis=1)

    half = nc // 2
    ahead = [mine] + [sketch_ref[lax.rem(c + k, nc)] for k in range(1, half + 1)]
    gram = dot_bf16(mine, jnp.concatenate(ahead, axis=1), ((0,), (0,)))
    for j in range(nd):
        gpart_ref[j] = gram[j * gram_rows : (j + 1) * gram_rows, :]
    started += exchange(
        "dp", d, nd, lambda j, p: gpart_ref.at[p], lambda j, p: gin_ref.at[j], s_gram, r_gram
    )
    pairs = nd // 2
    high, low = d // 2, d % 2
    mate = d + 1 - 2 * low
    cross = dot_bf16(responses, sketch, ((0,), (0,)))
    for j in range(nd):
        cpart_ref[j % 2, j // 2] = cross[j * cross_rows : (j + 1) * cross_rows, :]
    arrived("dp", d, nd, lambda j, p: gin_ref.at[j], s_gram, r_gram)
    total = gpart_ref[d]
    for j in range(1, nd):
        total = total + gin_ref[j]
    gsum_ref[c, d] = total
    started += gather("dp", d, nd, lambda i: gsum_ref.at[c, i], s_rows, r_rows, s_rows2, r_rows2)
    started.append(
        send("dp", mate, cpart_ref.at[1 - low], cmate_ref, s_mate.at[0], r_mate.at[0])
    )
    started += gather(
        "chan", c, nc, lambda i: gsum_ref.at[i], s_blocks, r_blocks, s_blocks2, r_blocks2
    )
    for first in range(nc):
        for k in range(half + 1):
            second = first + k
            lanes = slice(k * share, (k + 1) * share)
            if second < nc:
                for j in range(nd):
                    top = first * share + j * gram_rows
                    big_ref[top : top + gram_rows, second * share : (second + 1) * share] = gsum_ref[
                        first, j, :, lanes
                    ]
            elif k < half:
                for j in range(nd):
                    work_ref[j * gram_rows : (j + 1) * gram_rows, 0:share] = gsum_ref[first, j, :, lanes]
                second -= nc
                big_ref[
                    second * share : (second + 1) * share, first * share : (first + 1) * share
                ] = jnp.transpose(work_ref[0:share, 0:share])
    if share < BLOCK:
        full = big_ref[...]
        square = (size, size)
        above = lax.broadcasted_iota(jnp.int32, square, 1) > lax.broadcasted_iota(jnp.int32, square, 0)
        big_ref[...] = jnp.where(above, full, jnp.transpose(full))

    def between():
        expect("dp", mate, cmate_ref, s_mate.at[0], r_mate.at[0])
        cmate_ref[...] = cmate_ref[...] + cpart_ref[low]
        for j in range(1, pairs):
            place = lax.rem(high + j, pairs)
            send("dp", 2 * place + low, cmate_ref.at[place], cin_ref.at[j], s_cross.at[j], r_cross.at[j])

    eliminate(big_ref, work_ref, stack_ref, diag_ref, size, between)
    square = (size, size)
    row_of = lax.broadcasted_iota(jnp.int32, square, 0)
    lane_of = lax.broadcasted_iota(jnp.int32, square, 1)
    inverse = jnp.where(lane_of <= row_of, big_ref[...], 0.0)
    ih, im, il = split3(inverse)
    own = cmate_ref[high]
    for j in range(1, pairs):
        sender = 2 * lax.rem(high + pairs - j, pairs) + low
        expect("dp", sender, cin_ref.at[j], s_cross.at[j], r_cross.at[j])
        own = own + cin_ref[j]
    oh, om, ol = split3(own)
    inner = ((1,), (1,))
    coeffs = dot_bf16(oh, il, inner) + dot_bf16(om, im, inner) + dot_bf16(ol, ih, inner)
    coeffs = coeffs + dot_bf16(oh, im, inner) + dot_bf16(om, ih, inner)
    coeffs = (coeffs + dot_bf16(oh, ih, inner)).astype(BF16)
    outer = ((1,), (0,))
    mapped = dot_bf16(coeffs, il, outer) + dot_bf16(coeffs, im, outer)
    map_ref[d] = (mapped + dot_bf16(coeffs, ih, outer)).astype(BF16)
    started += gather("dp", d, nd, lambda i: map_ref.at[i], s_map, r_map, s_map2, r_map2)
    if last:
        scale = 1.0 / math.sqrt(total_rows)
        upper_ref[...] = jnp.where(lane_of >= row_of, big_ref[...], 0.0) * scale
        for b in range(size // BLOCK):
            at = slice(b * BLOCK, (b + 1) * BLOCK)
            upper_ref[at, at] = diag_ref[b] * scale
    for j in range(1, pairs):
        place = lax.rem(high + j, pairs)
        pltpu.make_async_remote_copy(
            src_ref=cmate_ref.at[place],
            dst_ref=cin_ref.at[j],
            send_sem=s_cross.at[j],
            recv_sem=r_cross.at[j],
            device_id={"dp": 2 * place + low},
            device_id_type=pl.DeviceIdType.MESH,
        ).wait_send()
    if cross_rows % 16 == 0:
        mapped = jnp.concatenate([map_ref[j] for j in range(nd)], axis=0)
    else:
        mapped = jnp.concatenate([map_ref[j].astype(F32) for j in range(nd)], axis=0).astype(BF16)
    restored = dot_bf16(sketch, mapped, ((1,), (1,)))
    if not last:
        restored = jnp.maximum(restored, 0.0)
    out_ref[...] = restored[0:rows, :].astype(BF16)
    for copy in started:
        copy.wait_send()


def first_kernel(nd, nc, total_rows, field_ref, weight_ref, probe_ref, out_ref, *rest):
    layer_kernel(nd, nc, False, total_rows, field_ref, weight_ref, probe_ref, out_ref, None, *rest)


def last_kernel(nd, nc, total_rows, *refs):
    layer_kernel(nd, nc, True, total_rows, *refs)


def layer(field, weight, probe, last):
    nd, nc = lax.axis_size("dp"), lax.axis_size("chan")
    rows, width = field.shape
    size = probe.shape[1]
    padded = -(-rows // 16) * 16
    share = size // nc
    gram_rows = share // nd
    gram_lanes = (nc // 2 + 1) * share
    cross_rows = width // nd
    restored = jax.ShapeDtypeStruct((rows, width), BF16)
    upper = jax.ShapeDtypeStruct((size, size), F32)
    chan_sems = pltpu.SemaphoreType.DMA((nc,))
    dp_sems = pltpu.SemaphoreType.DMA((nd,))
    return pl.pallas_call(
        functools.partial(last_kernel if last else first_kernel, nd, nc, rows * nd),
        out_shape=(restored, upper) if last else restored,
        scratch_shapes=[
            pltpu.VMEM((rows + 2 * PAD, width), F32),
            pltpu.VMEM((padded, width), BF16),
            pltpu.VMEM((nc, padded, share), BF16),
            pltpu.VMEM((nc, padded, share), BF16),
            pltpu.VMEM((nc, padded, share), BF16),
            pltpu.VMEM((nd, gram_rows, gram_lanes), F32),
            pltpu.VMEM((nd, gram_rows, gram_lanes), F32),
            pltpu.VMEM((nc, nd, gram_rows, gram_lanes), F32),
            pltpu.VMEM((2, nd // 2, cross_rows, size), F32),
            pltpu.VMEM((nd // 2, cross_rows, size), F32),
            pltpu.VMEM((nd // 2, cross_rows, size), F32),
            pltpu.VMEM((nd, cross_rows, size), BF16),
            pltpu.VMEM((size, size), F32),
            pltpu.VMEM((BLOCK, 2 * BLOCK), F32),
            pltpu.VMEM((6 * BLOCK, size), BF16),
            pltpu.VMEM((size // BLOCK, BLOCK, BLOCK), F32),
        ]
        + [chan_sems] * 10
        + [dp_sems] * 14,
        compiler_params=pltpu.CompilerParams(
            vmem_limit_bytes=VMEM_LIMIT, collective_id=1 if last else 0, has_side_effects=True
        ),
    )(field, weight, probe)


def per_device(inputs, conv_one, conv_two, probe_one, probe_two):
    activated = layer(inputs, conv_one, probe_one, False)
    return layer(activated, conv_two, probe_two, True)


def solution(mesh):
    in_specs = (
        P("dp", "chan"),
        P(None, None, "chan"),
        P(None, None, "chan"),
        P("chan", None),
        P("chan", None),
    )
    return jax.shard_map(
        per_device, mesh=mesh, in_specs=in_specs, out_specs=(P("dp", "chan"), P()), check_vma=False
    )
```

```python
import functools
import math

import jax
import jax.numpy as jnp
from jax import lax
from jax.experimental import pallas as pl
from jax.experimental.pallas import tpu as pltpu
from jax.sharding import PartitionSpec as P

SIDE = 7
PAD = 16
BLOCK = 128
PANEL = 16
F32 = jnp.float32
BF16 = jnp.bfloat16
VMEM_LIMIT = 48 * 1024 * 1024


def dot_f32(a, b, dims):
    return lax.dot_general(
        a, b, (dims, ((), ())), preferred_element_type=F32, precision=lax.Precision.HIGHEST
    )


def dot_bf16(a, b, dims):
    return lax.dot_general(a, b, (dims, ((), ())), preferred_element_type=F32)


def conv_into(field_ref, weight_ref, pad_ref, out_ref):
    rows, width = field_ref.shape
    group = weight_ref.shape[1]
    lanes = min(256, width)
    pad_ref[0:PAD, :] = jnp.zeros((PAD, width), F32)
    pad_ref[PAD + rows : PAD + rows + PAD, :] = jnp.zeros((PAD, width), F32)
    pad_ref[PAD : PAD + rows, :] = field_ref[...].astype(F32)
    place = lax.broadcasted_iota(jnp.int32, (rows, lanes), 0).astype(F32)
    pixel = place - (SIDE * SIDE) * jnp.floor((place + 0.5) * (1.0 / (SIDE * SIDE)))
    line = jnp.floor((pixel + 0.5) * (1.0 / SIDE))
    column = pixel - SIDE * line
    one, zero = jnp.ones((), F32), jnp.zeros((), F32)
    line_ok = (jnp.where(line > 0.5, one, zero), None, jnp.where(line < SIDE - 1.5, one, zero))
    column_ok = (jnp.where(column > 0.5, one, zero), None, jnp.where(column < SIDE - 1.5, one, zero))
    same = (
        lax.broadcasted_iota(jnp.int32, (lanes, lanes), 0) // group
        == lax.broadcasted_iota(jnp.int32, (lanes, lanes), 1) // group
    )
    for start in range(0, width, lanes):
        total = None
        for a in range(3):
            for b in range(3):
                shift = (a - 1) * SIDE + (b - 1)
                window = pad_ref[PAD + shift : PAD + shift + rows, start : start + lanes]
                if line_ok[a] is not None:
                    window = window * line_ok[a]
                if column_ok[b] is not None:
                    window = window * column_ok[b]
                small = weight_ref[3 * a + b, :, start : start + lanes]
                full = jnp.concatenate([small] * (lanes // group), axis=0)
                full = jnp.where(same, full, jnp.zeros((), BF16))
                part = dot_bf16(window.astype(BF16), full, ((1,), (0,)))
                total = part if total is None else total + part
        out_ref[0:rows, start : start + lanes] = total.astype(BF16)
    if out_ref.shape[0] > rows:
        out_ref[rows:, :] = jnp.zeros((out_ref.shape[0] - rows, width), BF16)


def split3(x):
    high = x.astype(BF16)
    rest = x - high.astype(F32)
    middle = rest.astype(BF16)
    low = (rest - middle.astype(F32)).astype(BF16)
    return high, middle, low


def stack_first(x, axis):
    h, m, l = split3(x)
    return jnp.concatenate([h, h, m, h, l, m], axis=axis)


def stack_second(x):
    h, m, l = split3(x)
    return jnp.concatenate([h, m, h, l, h, m], axis=0)


def eliminate_block(work_ref):
    row_of = lax.broadcasted_iota(jnp.int32, (PANEL, BLOCK), 0)
    for panel in range(BLOCK // PANEL):
        top = panel * PANEL
        left = work_ref[top : top + PANEL, 0:BLOCK]
        right = work_ref[top : top + PANEL, BLOCK : 2 * BLOCK]
        cols = [
            jnp.broadcast_to(left[:, top + k : top + k + 1], (PANEL, BLOCK)) for k in range(PANEL)
        ]
        scale = jnp.zeros((PANEL, BLOCK), F32)
        for i in range(PANEL):
            pivot = jnp.broadcast_to(cols[i][i : i + 1, :], (PANEL, BLOCK))
            root = lax.rsqrt(pivot)
            scale = jnp.where(row_of == i, root, scale)
            if i < PANEL - 1:
                below = jnp.where(row_of > i, cols[i], 0.0)
                ahead = below * cols[i + 1][i : i + 1, :]
                square = root * root
                cols[i + 1] = cols[i + 1] - ahead * square
                factor = below * square
                for k in range(i + 2, PANEL):
                    cols[k] = cols[k] - factor * cols[k][i : i + 1, :]
                left = left - factor * left[i : i + 1, :]
                right = right - factor * right[i : i + 1, :]
        left = left * scale
        right = right * scale
        lane_of = lax.broadcasted_iota(jnp.int32, (PANEL, BLOCK), 1)
        left = jnp.where(lane_of >= top + row_of, left, 0.0)
        work_ref[top : top + PANEL, 0:BLOCK] = left
        work_ref[top : top + PANEL, BLOCK : 2 * BLOCK] = right
        if top + PANEL < BLOCK:
            rest = top + PANEL
            second = jnp.concatenate([stack_second(left), stack_second(right)], axis=1)
            update = dot_bf16(stack_first(left, 0), second, ((0,), (0,)))
            work_ref[rest:BLOCK, :] = work_ref[rest:BLOCK, :] - update[rest:BLOCK, :]


def eliminate(big_ref, work_ref, stack_ref, diag_ref, size, between):
    blocks = size // BLOCK
    square = (BLOCK, BLOCK)
    eye = jnp.where(
        lax.broadcasted_iota(jnp.int32, square, 0) == lax.broadcasted_iota(jnp.int32, square, 1),
        1.0,
        0.0,
    )

    @pl.loop(0, blocks)
    def _(b):
        for step, task in enumerate(between):
            pl.when(b == step + 1)(task)
        at = pl.ds(pl.multiple_of(b * BLOCK, BLOCK), BLOCK)
        work_ref[:, 0:BLOCK] = big_ref[at, at]
        work_ref[:, BLOCK : 2 * BLOCK] = eye
        eliminate_block(work_ref)
        diag_ref[b] = work_ref[:, 0:BLOCK]
        inverse = work_ref[:, BLOCK : 2 * BLOCK]
        big_ref[at, at] = eye
        row = dot_bf16(stack_first(inverse, 1), stack_second(big_ref[at, :]), ((1,), (0,)))
        big_ref[at, :] = row
        stack_ref[...] = stack_second(row)

        @pl.loop(b + 1, blocks)
        def _(other):
            to = pl.ds(pl.multiple_of(other * BLOCK, BLOCK), BLOCK)
            big_ref[to, at] = jnp.zeros(square, F32)
            factor = stack_first(big_ref[at, to], 0)
            big_ref[to, :] = big_ref[to, :] - dot_bf16(factor, stack_ref[...], ((0,), (0,)))


def exchange(axis, me, count, source, target, send_sem, recv_sem):
    copies = []
    for j in range(1, count):
        peer = lax.rem(me + j, count)
        copy = pltpu.make_async_remote_copy(
            src_ref=source(j, peer),
            dst_ref=target(j, peer),
            send_sem=send_sem.at[j],
            recv_sem=recv_sem.at[j],
            device_id={axis: peer},
            device_id_type=pl.DeviceIdType.MESH,
        )
        copy.start()
        copies.append(copy)
    return copies


def arrived(axis, me, count, target, send_sem, recv_sem):
    for j in range(1, count):
        sender = lax.rem(me + count - j, count)
        pltpu.make_async_remote_copy(
            src_ref=target(j, sender),
            dst_ref=target(j, sender),
            send_sem=send_sem.at[j],
            recv_sem=recv_sem.at[j],
            device_id={axis: sender},
            device_id_type=pl.DeviceIdType.MESH,
        ).wait_recv()


def send(axis, peer, source, target, send_sem, recv_sem):
    copy = pltpu.make_async_remote_copy(
        src_ref=source,
        dst_ref=target,
        send_sem=send_sem,
        recv_sem=recv_sem,
        device_id={axis: peer},
        device_id_type=pl.DeviceIdType.MESH,
    )
    copy.start()
    return copy


def expect(axis, sender, target, send_sem, recv_sem):
    pltpu.make_async_remote_copy(
        src_ref=target,
        dst_ref=target,
        send_sem=send_sem,
        recv_sem=recv_sem,
        device_id={axis: sender},
        device_id_type=pl.DeviceIdType.MESH,
    ).wait_recv()


def gather(axis, me, count, slot, far_send, far_recv, mate_send, mate_recv):
    high, low = me // 2, me % 2
    mate = me + 1 - 2 * low
    pairs = count // 2
    copies = [
        send(axis, 2 * lax.rem(high + j, pairs) + low, slot(me), slot(me), far_send.at[j], far_recv.at[j])
        for j in range(1, pairs)
    ]
    copies.append(send(axis, mate, slot(me), slot(me), mate_send.at[0], mate_recv.at[0]))
    for j in range(1, pairs):
        sender = 2 * lax.rem(high + pairs - j, pairs) + low
        expect(axis, sender, slot(sender), far_send.at[j], far_recv.at[j])
        copies.append(send(axis, mate, slot(sender), slot(sender), mate_send.at[j], mate_recv.at[j]))
    expect(axis, mate, slot(mate), mate_send.at[0], mate_recv.at[0])
    for j in range(1, pairs):
        origin = 2 * lax.rem(high + pairs - j, pairs) + 1 - low
        expect(axis, mate, slot(origin), mate_send.at[j], mate_recv.at[j])
    return copies


def gather_rows(d, nd, c, nc, slot, far, mate_sems, chan_far, chan_mate, middle):
    high, low = d // 2, d % 2
    mate = d + 1 - 2 * low
    pairs = nd // 2
    chan_high, chan_low = c // 2, c % 2
    chan_other = c + 1 - 2 * chan_low
    chan_pairs = nc // 2
    copies = []

    def over_chan(order, piece):
        ref = slot(c, piece)
        for j in range(1, chan_pairs):
            peer = 2 * lax.rem(chan_high + j, chan_pairs) + chan_low
            copies.append(send("chan", peer, ref, ref, chan_far[0].at[order, j], chan_far[1].at[order, j]))
        copies.append(send("chan", chan_other, ref, ref, chan_mate[0].at[order, 0], chan_mate[1].at[order, 0]))

    mine = slot(c, d)
    for j in range(1, pairs):
        peer = 2 * lax.rem(high + j, pairs) + low
        copies.append(send("dp", peer, mine, mine, far[0].at[j], far[1].at[j]))
    copies.append(send("dp", mate, mine, mine, mate_sems[0].at[0], mate_sems[1].at[0]))
    over_chan(0, d)
    pieces = [d, mate]
    expect("dp", mate, slot(c, mate), mate_sems[0].at[0], mate_sems[1].at[0])
    over_chan(1, mate)
    for j in range(1, pairs):
        sender = 2 * lax.rem(high + pairs - j, pairs) + low
        piece = slot(c, sender)
        expect("dp", sender, piece, far[0].at[j], far[1].at[j])
        copies.append(send("dp", mate, piece, piece, mate_sems[0].at[j], mate_sems[1].at[j]))
        over_chan(2 * j, sender)
        pieces.append(sender)
        origin = 2 * lax.rem(high + pairs - j, pairs) + 1 - low
        expect("dp", mate, slot(c, origin), mate_sems[0].at[j], mate_sems[1].at[j])
        over_chan(2 * j + 1, origin)
        pieces.append(origin)
    middle()
    for order, piece in enumerate(pieces):
        for j in range(1, chan_pairs):
            sender = 2 * lax.rem(chan_high + chan_pairs - j, chan_pairs) + chan_low
            ref = slot(sender, piece)
            expect("chan", sender, ref, chan_far[0].at[order, j], chan_far[1].at[order, j])
            copies.append(
                send("chan", chan_other, ref, ref, chan_mate[0].at[order, j], chan_mate[1].at[order, j])
            )
    for order, piece in enumerate(pieces):
        for j in range(chan_pairs):
            origin = 2 * lax.rem(chan_high + chan_pairs - j, chan_pairs) + 1 - chan_low
            expect(
                "chan", chan_other, slot(origin, piece), chan_mate[0].at[order, j], chan_mate[1].at[order, j]
            )
    return copies


def layer_kernel(
    nd, nc, last, total_rows,
    field_any, weight_any, probe_any, out_ref, upper_ref,
    pad_ref, resp_ref, part_ref, part_in_ref, sketch_ref, gpart_ref, gin_ref, gsum_ref,
    cpart_ref, cmate_ref, cin_ref, map_ref, big_ref, work_ref, stack_ref, diag_ref,
    s_part, r_part, s_sketch, r_sketch, s_sketch2, r_sketch2,
    s_gram, r_gram, s_rows, r_rows, s_rows2, r_rows2, s_mate, r_mate, s_cross, r_cross,
    s_map, r_map, s_map2, r_map2, s_blocks, r_blocks, s_blocks2, r_blocks2, s_load,
    field_ref, weight_ref, probe_ref,
):
    loads = [
        pltpu.make_async_copy(source, target, s_load.at[k])
        for k, (source, target) in enumerate(
            ((field_any, field_ref), (weight_any, weight_ref), (probe_any, probe_ref))
        )
    ]
    for load in loads:
        load.start()
    d = lax.axis_index("dp")
    c = lax.axis_index("chan")
    rows, width = field_ref.shape
    size = probe_ref.shape[1]
    padded = resp_ref.shape[0]
    share = size // nc
    gram_rows = share // nd
    cross_rows = width // nd

    barrier = pltpu.get_barrier_semaphore()
    for j in range(1, nd):
        pl.semaphore_signal(
            barrier, inc=1, device_id={"dp": lax.rem(d + j, nd)}, device_id_type=pl.DeviceIdType.MESH
        )
    for j in range(1, nc):
        pl.semaphore_signal(
            barrier, inc=1, device_id={"chan": lax.rem(c + j, nc)}, device_id_type=pl.DeviceIdType.MESH
        )

    big_ref[...] = jnp.zeros((size, size), F32)
    loads[0].wait()
    loads[1].wait()
    conv_into(field_ref, weight_ref, pad_ref, resp_ref)
    responses = resp_ref[...]
    loads[2].wait()
    for j in range(nc):
        block = dot_bf16(responses, probe_ref[:, j * share : (j + 1) * share], ((1,), (0,)))
        part_ref[j] = block.astype(BF16)
    pl.semaphore_wait(barrier, nd + nc - 2)

    started = exchange(
        "chan", c, nc, lambda j, p: part_ref.at[p], lambda j, p: part_in_ref.at[j], s_part, r_part
    )
    arrived("chan", c, nc, lambda j, p: part_in_ref.at[j], s_part, r_part)
    mine = part_ref[c].astype(F32)
    for j in range(1, nc):
        mine = mine + part_in_ref[j].astype(F32)
    mine = mine.astype(BF16)
    sketch_ref[c] = mine
    started += gather(
        "chan", c, nc, lambda i: sketch_ref.at[i], s_sketch, r_sketch, s_sketch2, r_sketch2
    )
    sketch = jnp.concatenate([sketch_ref[j] for j in range(nc)], axis=1)

    half = nc // 2
    ahead = [mine] + [sketch_ref[lax.rem(c + k, nc)] for k in range(1, half + 1)]
    gram = dot_bf16(mine, jnp.concatenate(ahead, axis=1), ((0,), (0,)))
    for j in range(nd):
        gpart_ref[j] = gram[j * gram_rows : (j + 1) * gram_rows, :]
    started += exchange(
        "dp", d, nd, lambda j, p: gpart_ref.at[p], lambda j, p: gin_ref.at[j], s_gram, r_gram
    )
    pairs = nd // 2
    high, low = d // 2, d % 2
    mate = d + 1 - 2 * low
    cross = dot_bf16(responses, sketch, ((0,), (0,)))
    for j in range(nd):
        cpart_ref[j % 2, j // 2] = cross[j * cross_rows : (j + 1) * cross_rows, :]
    arrived("dp", d, nd, lambda j, p: gin_ref.at[j], s_gram, r_gram)
    total = gpart_ref[d]
    for j in range(1, nd):
        total = total + gin_ref[j]
    gsum_ref[c, d] = total
    places = [lax.rem(high + j, pairs) for j in range(1, pairs)] + [high]

    def middle():
        for j, place in enumerate(places):
            started.append(
                send("dp", mate, cpart_ref.at[1 - low, place], cmate_ref.at[place], s_mate.at[j], r_mate.at[j])
            )

    def add_mate(j):
        place = places[j]
        expect("dp", mate, cmate_ref.at[place], s_mate.at[j], r_mate.at[j])
        cmate_ref[place] = cmate_ref[place] + cpart_ref[low, place]

    started += gather_rows(
        d, nd, c, nc, lambda k, i: gsum_ref.at[k, i],
        (s_rows, r_rows), (s_rows2, r_rows2), (s_blocks, r_blocks), (s_blocks2, r_blocks2), middle,
    )
    for first in range(nc):
        for k in range(half + 1):
            second = first + k
            lanes = slice(k * share, (k + 1) * share)
            if second < nc:
                for j in range(nd):
                    top = first * share + j * gram_rows
                    big_ref[top : top + gram_rows, second * share : (second + 1) * share] = gsum_ref[
                        first, j, :, lanes
                    ]
            elif k < half:
                for j in range(nd):
                    work_ref[j * gram_rows : (j + 1) * gram_rows, 0:share] = gsum_ref[first, j, :, lanes]
                second -= nc
                big_ref[
                    second * share : (second + 1) * share, first * share : (first + 1) * share
                ] = jnp.transpose(work_ref[0:share, 0:share])
    if share < BLOCK:
        full = big_ref[...]
        square = (size, size)
        above = lax.broadcasted_iota(jnp.int32, square, 1) > lax.broadcasted_iota(jnp.int32, square, 0)
        big_ref[...] = jnp.where(above, full, jnp.transpose(full))

    def pass_on(first, end):
        for j in range(first, end):
            add_mate(j)
            place = places[j]
            send(
                "dp", 2 * place + low, cmate_ref.at[place], cin_ref.at[j + 1],
                s_cross.at[j + 1], r_cross.at[j + 1],
            )

    early = pairs // 2
    between = (lambda: pass_on(0, early), lambda: pass_on(early, pairs - 1))
    eliminate(big_ref, work_ref, stack_ref, diag_ref, size, between)
    square = (size, size)
    row_of = lax.broadcasted_iota(jnp.int32, square, 0)
    lane_of = lax.broadcasted_iota(jnp.int32, square, 1)
    inverse = jnp.where(lane_of <= row_of, big_ref[...], 0.0)
    ih, im, il = split3(inverse)
    add_mate(pairs - 1)
    own = cmate_ref[high]
    for j in range(1, pairs):
        sender = 2 * lax.rem(high + pairs - j, pairs) + low
        expect("dp", sender, cin_ref.at[j], s_cross.at[j], r_cross.at[j])
        own = own + cin_ref[j]
    oh, om, ol = split3(own)
    inner = ((1,), (1,))
    coeffs = dot_bf16(oh, il, inner) + dot_bf16(om, im, inner) + dot_bf16(ol, ih, inner)
    coeffs = coeffs + dot_bf16(oh, im, inner) + dot_bf16(om, ih, inner)
    coeffs = (coeffs + dot_bf16(oh, ih, inner)).astype(BF16)
    outer = ((1,), (0,))
    mapped = dot_bf16(coeffs, il, outer) + dot_bf16(coeffs, im, outer)
    map_ref[d] = (mapped + dot_bf16(coeffs, ih, outer)).astype(BF16)
    started += gather("dp", d, nd, lambda i: map_ref.at[i], s_map, r_map, s_map2, r_map2)
    if last:
        scale = 1.0 / math.sqrt(total_rows)
        upper_ref[...] = jnp.where(lane_of >= row_of, big_ref[...], 0.0) * scale
        for b in range(size // BLOCK):
            at = slice(b * BLOCK, (b + 1) * BLOCK)
            upper_ref[at, at] = diag_ref[b] * scale
    for j in range(1, pairs):
        place = lax.rem(high + j, pairs)
        pltpu.make_async_remote_copy(
            src_ref=cmate_ref.at[place],
            dst_ref=cin_ref.at[j],
            send_sem=s_cross.at[j],
            recv_sem=r_cross.at[j],
            device_id={"dp": 2 * place + low},
            device_id_type=pl.DeviceIdType.MESH,
        ).wait_send()
    if cross_rows % 16 == 0:
        mapped = jnp.concatenate([map_ref[j] for j in range(nd)], axis=0)
    else:
        mapped = jnp.concatenate([map_ref[j].astype(F32) for j in range(nd)], axis=0).astype(BF16)
    restored = dot_bf16(sketch, mapped, ((1,), (1,)))
    if not last:
        restored = jnp.maximum(restored, 0.0)
    out_ref[...] = restored[0:rows, :].astype(BF16)
    for copy in started:
        copy.wait_send()


def first_kernel(nd, nc, total_rows, field_ref, weight_ref, probe_ref, out_ref, *rest):
    layer_kernel(nd, nc, False, total_rows, field_ref, weight_ref, probe_ref, out_ref, None, *rest)


def last_kernel(nd, nc, total_rows, *refs):
    layer_kernel(nd, nc, True, total_rows, *refs)


def layer(field, weight, probe, last):
    nd, nc = lax.axis_size("dp"), lax.axis_size("chan")
    rows, width = field.shape
    size = probe.shape[1]
    padded = -(-rows // 16) * 16
    share = size // nc
    gram_rows = share // nd
    gram_lanes = (nc // 2 + 1) * share
    cross_rows = width // nd
    restored = jax.ShapeDtypeStruct((rows, width), BF16)
    upper = jax.ShapeDtypeStruct((size, size), F32)
    chan_sems = pltpu.SemaphoreType.DMA((nc,))
    dp_sems = pltpu.SemaphoreType.DMA((nd,))
    return pl.pallas_call(
        functools.partial(last_kernel if last else first_kernel, nd, nc, rows * nd),
        out_shape=(restored, upper) if last else restored,
        in_specs=[pl.BlockSpec(memory_space=pl.ANY)] * 3,
        scratch_shapes=[
            pltpu.VMEM((rows + 2 * PAD, width), F32),
            pltpu.VMEM((padded, width), BF16),
            pltpu.VMEM((nc, padded, share), BF16),
            pltpu.VMEM((nc, padded, share), BF16),
            pltpu.VMEM((nc, padded, share), BF16),
            pltpu.VMEM((nd, gram_rows, gram_lanes), F32),
            pltpu.VMEM((nd, gram_rows, gram_lanes), F32),
            pltpu.VMEM((nc, nd, gram_rows, gram_lanes), F32),
            pltpu.VMEM((2, nd // 2, cross_rows, size), F32),
            pltpu.VMEM((nd // 2, cross_rows, size), F32),
            pltpu.VMEM((nd // 2, cross_rows, size), F32),
            pltpu.VMEM((nd, cross_rows, size), BF16),
            pltpu.VMEM((size, size), F32),
            pltpu.VMEM((BLOCK, 2 * BLOCK), F32),
            pltpu.VMEM((6 * BLOCK, size), BF16),
            pltpu.VMEM((size // BLOCK, BLOCK, BLOCK), F32),
        ]
        + [chan_sems] * 6
        + [dp_sems] * 14
        + [pltpu.SemaphoreType.DMA((nd, nc // 2))] * 4
        + [
            pltpu.SemaphoreType.DMA((3,)),
            pltpu.VMEM(field.shape, BF16),
            pltpu.VMEM(weight.shape, BF16),
            pltpu.VMEM(probe.shape, BF16),
        ],
        compiler_params=pltpu.CompilerParams(
            vmem_limit_bytes=VMEM_LIMIT, collective_id=1 if last else 0, has_side_effects=True
        ),
    )(field, weight, probe)


def per_device(inputs, conv_one, conv_two, probe_one, probe_two):
    activated = layer(inputs, conv_one, probe_one, False)
    return layer(activated, conv_two, probe_two, True)


def solution(mesh):
    in_specs = (
        P("dp", "chan"),
        P(None, None, "chan"),
        P(None, None, "chan"),
        P("chan", None),
        P("chan", None),
    )
    return jax.shard_map(
        per_device, mesh=mesh, in_specs=in_specs, out_specs=(P("dp", "chan"), P()), check_vma=False
    )
```

```python
import functools
import math

import jax
import jax.numpy as jnp
from jax import lax
from jax.experimental import pallas as pl
from jax.experimental.pallas import tpu as pltpu
from jax.sharding import PartitionSpec as P

SIDE = 7
PAD = 16
BLOCK = 128
PANEL = 16
F32 = jnp.float32
BF16 = jnp.bfloat16
VMEM_LIMIT = 48 * 1024 * 1024


def dot_f32(a, b, dims):
    return lax.dot_general(
        a, b, (dims, ((), ())), preferred_element_type=F32, precision=lax.Precision.HIGHEST
    )


def dot_bf16(a, b, dims):
    return lax.dot_general(a, b, (dims, ((), ())), preferred_element_type=F32)


def conv_into(field_ref, weight_ref, pad_ref, out_ref):
    rows, width = field_ref.shape
    group = weight_ref.shape[1]
    lanes = min(256, width)
    pad_ref[0:PAD, :] = jnp.zeros((PAD, width), F32)
    pad_ref[PAD + rows : PAD + rows + PAD, :] = jnp.zeros((PAD, width), F32)
    pad_ref[PAD : PAD + rows, :] = field_ref[...].astype(F32)
    place = lax.broadcasted_iota(jnp.int32, (rows, lanes), 0).astype(F32)
    pixel = place - (SIDE * SIDE) * jnp.floor((place + 0.5) * (1.0 / (SIDE * SIDE)))
    line = jnp.floor((pixel + 0.5) * (1.0 / SIDE))
    column = pixel - SIDE * line
    one, zero = jnp.ones((), F32), jnp.zeros((), F32)
    line_ok = (jnp.where(line > 0.5, one, zero), None, jnp.where(line < SIDE - 1.5, one, zero))
    column_ok = (jnp.where(column > 0.5, one, zero), None, jnp.where(column < SIDE - 1.5, one, zero))
    same = (
        lax.broadcasted_iota(jnp.int32, (lanes, lanes), 0) // group
        == lax.broadcasted_iota(jnp.int32, (lanes, lanes), 1) // group
    )
    for start in range(0, width, lanes):
        total = None
        for a in range(3):
            for b in range(3):
                shift = (a - 1) * SIDE + (b - 1)
                window = pad_ref[PAD + shift : PAD + shift + rows, start : start + lanes]
                if line_ok[a] is not None:
                    window = window * line_ok[a]
                if column_ok[b] is not None:
                    window = window * column_ok[b]
                small = weight_ref[3 * a + b, :, start : start + lanes]
                full = jnp.concatenate([small] * (lanes // group), axis=0)
                full = jnp.where(same, full, jnp.zeros((), BF16))
                part = dot_bf16(window.astype(BF16), full, ((1,), (0,)))
                total = part if total is None else total + part
        out_ref[0:rows, start : start + lanes] = total.astype(BF16)
    if out_ref.shape[0] > rows:
        out_ref[rows:, :] = jnp.zeros((out_ref.shape[0] - rows, width), BF16)


def split3(x):
    high = x.astype(BF16)
    rest = x - high.astype(F32)
    middle = rest.astype(BF16)
    low = (rest - middle.astype(F32)).astype(BF16)
    return high, middle, low


def stack_first(x, axis):
    h, m, l = split3(x)
    return jnp.concatenate([h, h, m, h, l, m], axis=axis)


def stack_second(x):
    h, m, l = split3(x)
    return jnp.concatenate([h, m, h, l, h, m], axis=0)


def eliminate_block(work_ref):
    row_of = lax.broadcasted_iota(jnp.int32, (PANEL, BLOCK), 0)
    for panel in range(BLOCK // PANEL):
        top = panel * PANEL
        left = work_ref[top : top + PANEL, 0:BLOCK]
        right = work_ref[top : top + PANEL, BLOCK : 2 * BLOCK]
        cols = [
            jnp.broadcast_to(left[:, top + k : top + k + 1], (PANEL, BLOCK)) for k in range(PANEL)
        ]
        scale = jnp.zeros((PANEL, BLOCK), F32)
        for i in range(PANEL):
            pivot = jnp.broadcast_to(cols[i][i : i + 1, :], (PANEL, BLOCK))
            root = lax.rsqrt(pivot)
            scale = jnp.where(row_of == i, root, scale)
            if i < PANEL - 1:
                below = jnp.where(row_of > i, cols[i], 0.0)
                ahead = below * cols[i + 1][i : i + 1, :]
                square = root * root
                cols[i + 1] = cols[i + 1] - ahead * square
                factor = below * square
                for k in range(i + 2, PANEL):
                    cols[k] = cols[k] - factor * cols[k][i : i + 1, :]
                left = left - factor * left[i : i + 1, :]
                right = right - factor * right[i : i + 1, :]
        left = left * scale
        right = right * scale
        lane_of = lax.broadcasted_iota(jnp.int32, (PANEL, BLOCK), 1)
        left = jnp.where(lane_of >= top + row_of, left, 0.0)
        work_ref[top : top + PANEL, 0:BLOCK] = left
        work_ref[top : top + PANEL, BLOCK : 2 * BLOCK] = right
        if top + PANEL < BLOCK:
            rest = top + PANEL
            second = jnp.concatenate([stack_second(left), stack_second(right)], axis=1)
            update = dot_bf16(stack_first(left, 0), second, ((0,), (0,)))
            work_ref[rest:BLOCK, :] = work_ref[rest:BLOCK, :] - update[rest:BLOCK, :]


def eliminate(big_ref, work_ref, stack_ref, diag_ref, size):
    blocks = size // BLOCK
    square = (BLOCK, BLOCK)
    eye = jnp.where(
        lax.broadcasted_iota(jnp.int32, square, 0) == lax.broadcasted_iota(jnp.int32, square, 1),
        1.0,
        0.0,
    )

    @pl.loop(0, blocks)
    def _(b):
        at = pl.ds(pl.multiple_of(b * BLOCK, BLOCK), BLOCK)
        work_ref[:, 0:BLOCK] = big_ref[at, at]
        work_ref[:, BLOCK : 2 * BLOCK] = eye
        eliminate_block(work_ref)
        diag_ref[b] = work_ref[:, 0:BLOCK]
        inverse = work_ref[:, BLOCK : 2 * BLOCK]
        big_ref[at, at] = eye
        row = dot_bf16(stack_first(inverse, 1), stack_second(big_ref[at, :]), ((1,), (0,)))
        big_ref[at, :] = row
        stack_ref[...] = stack_second(row)

        @pl.loop(b + 1, blocks)
        def _(other):
            to = pl.ds(pl.multiple_of(other * BLOCK, BLOCK), BLOCK)
            big_ref[to, at] = jnp.zeros(square, F32)
            factor = stack_first(big_ref[at, to], 0)
            big_ref[to, :] = big_ref[to, :] - dot_bf16(factor, stack_ref[...], ((0,), (0,)))


def exchange(axis, me, count, source, target, send_sem, recv_sem):
    copies = []
    for j in range(1, count):
        peer = lax.rem(me + j, count)
        copy = pltpu.make_async_remote_copy(
            src_ref=source(j, peer),
            dst_ref=target(j, peer),
            send_sem=send_sem.at[j],
            recv_sem=recv_sem.at[j],
            device_id={axis: peer},
            device_id_type=pl.DeviceIdType.MESH,
        )
        copy.start()
        copies.append(copy)
    return copies


def arrived(axis, me, count, target, send_sem, recv_sem):
    for j in range(1, count):
        sender = lax.rem(me + count - j, count)
        pltpu.make_async_remote_copy(
            src_ref=target(j, sender),
            dst_ref=target(j, sender),
            send_sem=send_sem.at[j],
            recv_sem=recv_sem.at[j],
            device_id={axis: sender},
            device_id_type=pl.DeviceIdType.MESH,
        ).wait_recv()


def send(axis, peer, source, target, send_sem, recv_sem):
    copy = pltpu.make_async_remote_copy(
        src_ref=source,
        dst_ref=target,
        send_sem=send_sem,
        recv_sem=recv_sem,
        device_id={axis: peer},
        device_id_type=pl.DeviceIdType.MESH,
    )
    copy.start()
    return copy


def expect(axis, sender, target, send_sem, recv_sem):
    pltpu.make_async_remote_copy(
        src_ref=target,
        dst_ref=target,
        send_sem=send_sem,
        recv_sem=recv_sem,
        device_id={axis: sender},
        device_id_type=pl.DeviceIdType.MESH,
    ).wait_recv()


def gather(axis, me, count, slot, far_send, far_recv, mate_send, mate_recv):
    high, low = me // 2, me % 2
    mate = me + 1 - 2 * low
    pairs = count // 2
    copies = [
        send(axis, 2 * lax.rem(high + j, pairs) + low, slot(me), slot(me), far_send.at[j], far_recv.at[j])
        for j in range(1, pairs)
    ]
    copies.append(send(axis, mate, slot(me), slot(me), mate_send.at[0], mate_recv.at[0]))
    for j in range(1, pairs):
        sender = 2 * lax.rem(high + pairs - j, pairs) + low
        expect(axis, sender, slot(sender), far_send.at[j], far_recv.at[j])
        copies.append(send(axis, mate, slot(sender), slot(sender), mate_send.at[j], mate_recv.at[j]))
    expect(axis, mate, slot(mate), mate_send.at[0], mate_recv.at[0])
    for j in range(1, pairs):
        origin = 2 * lax.rem(high + pairs - j, pairs) + 1 - low
        expect(axis, mate, slot(origin), mate_send.at[j], mate_recv.at[j])
    return copies


def gather_rows(d, nd, c, nc, slot, far, mate_sems, chan_far, chan_mate):
    high, low = d // 2, d % 2
    mate = d + 1 - 2 * low
    pairs = nd // 2
    chan_high, chan_low = c // 2, c % 2
    chan_other = c + 1 - 2 * chan_low
    chan_pairs = nc // 2
    copies = []

    def over_chan(order, piece):
        ref = slot(c, piece)
        for j in range(1, chan_pairs):
            peer = 2 * lax.rem(chan_high + j, chan_pairs) + chan_low
            copies.append(send("chan", peer, ref, ref, chan_far[0].at[order, j], chan_far[1].at[order, j]))
        copies.append(send("chan", chan_other, ref, ref, chan_mate[0].at[order, 0], chan_mate[1].at[order, 0]))

    mine = slot(c, d)
    for j in range(1, pairs):
        peer = 2 * lax.rem(high + j, pairs) + low
        copies.append(send("dp", peer, mine, mine, far[0].at[j], far[1].at[j]))
    copies.append(send("dp", mate, mine, mine, mate_sems[0].at[0], mate_sems[1].at[0]))
    over_chan(0, d)
    pieces = [d, mate]
    expect("dp", mate, slot(c, mate), mate_sems[0].at[0], mate_sems[1].at[0])
    over_chan(1, mate)
    for j in range(1, pairs):
        sender = 2 * lax.rem(high + pairs - j, pairs) + low
        piece = slot(c, sender)
        expect("dp", sender, piece, far[0].at[j], far[1].at[j])
        copies.append(send("dp", mate, piece, piece, mate_sems[0].at[j], mate_sems[1].at[j]))
        over_chan(2 * j, sender)
        pieces.append(sender)
        origin = 2 * lax.rem(high + pairs - j, pairs) + 1 - low
        expect("dp", mate, slot(c, origin), mate_sems[0].at[j], mate_sems[1].at[j])
        over_chan(2 * j + 1, origin)
        pieces.append(origin)
    for order, piece in enumerate(pieces):
        for j in range(1, chan_pairs):
            sender = 2 * lax.rem(chan_high + chan_pairs - j, chan_pairs) + chan_low
            ref = slot(sender, piece)
            expect("chan", sender, ref, chan_far[0].at[order, j], chan_far[1].at[order, j])
            copies.append(
                send("chan", chan_other, ref, ref, chan_mate[0].at[order, j], chan_mate[1].at[order, j])
            )
    for order, piece in enumerate(pieces):
        for j in range(chan_pairs):
            origin = 2 * lax.rem(chan_high + chan_pairs - j, chan_pairs) + 1 - chan_low
            expect(
                "chan", chan_other, slot(origin, piece), chan_mate[0].at[order, j], chan_mate[1].at[order, j]
            )
    return copies


def layer_kernel(
    nd, nc, last, total_rows,
    field_any, weight_any, probe_any, out_ref, upper_ref,
    pad_ref, resp_ref, part_ref, part_in_ref, sketch_ref, gpart_ref, gin_ref, gsum_ref,
    cpart_ref, cmate_ref, cin_ref, map_ref, big_ref, work_ref, stack_ref, diag_ref,
    s_part, r_part, s_sketch, r_sketch, s_sketch2, r_sketch2,
    s_gram, r_gram, s_rows, r_rows, s_rows2, r_rows2, s_mate, r_mate, s_cross, r_cross,
    s_map, r_map, s_map2, r_map2, s_blocks, r_blocks, s_blocks2, r_blocks2, s_load,
    field_ref, weight_ref, probe_ref,
):
    loads = [
        pltpu.make_async_copy(source, target, s_load.at[k])
        for k, (source, target) in enumerate(
            ((field_any, field_ref), (weight_any, weight_ref), (probe_any, probe_ref))
        )
    ]
    for load in loads:
        load.start()
    d = lax.axis_index("dp")
    c = lax.axis_index("chan")
    rows, width = field_ref.shape
    size = probe_ref.shape[1]
    padded = resp_ref.shape[0]
    share = size // nc
    gram_rows = share // nd
    cross_rows = width // nd

    barrier = pltpu.get_barrier_semaphore()
    for j in range(1, nd):
        pl.semaphore_signal(
            barrier, inc=1, device_id={"dp": lax.rem(d + j, nd)}, device_id_type=pl.DeviceIdType.MESH
        )
    for j in range(1, nc):
        pl.semaphore_signal(
            barrier, inc=1, device_id={"chan": lax.rem(c + j, nc)}, device_id_type=pl.DeviceIdType.MESH
        )

    big_ref[...] = jnp.zeros((size, size), F32)
    loads[0].wait()
    loads[1].wait()
    conv_into(field_ref, weight_ref, pad_ref, resp_ref)
    responses = resp_ref[...]
    loads[2].wait()
    for j in range(nc):
        block = dot_bf16(responses, probe_ref[:, j * share : (j + 1) * share], ((1,), (0,)))
        part_ref[j] = block.astype(BF16)
    pl.semaphore_wait(barrier, nd + nc - 2)

    started = exchange(
        "chan", c, nc, lambda j, p: part_ref.at[p], lambda j, p: part_in_ref.at[j], s_part, r_part
    )
    arrived("chan", c, nc, lambda j, p: part_in_ref.at[j], s_part, r_part)
    mine = part_ref[c].astype(F32)
    for j in range(1, nc):
        mine = mine + part_in_ref[j].astype(F32)
    mine = mine.astype(BF16)
    sketch_ref[c] = mine
    started += gather(
        "chan", c, nc, lambda i: sketch_ref.at[i], s_sketch, r_sketch, s_sketch2, r_sketch2
    )
    sketch = jnp.concatenate([sketch_ref[j] for j in range(nc)], axis=1)

    half = nc // 2
    ahead = [mine] + [sketch_ref[lax.rem(c + k, nc)] for k in range(1, half + 1)]
    gram = dot_bf16(mine, jnp.concatenate(ahead, axis=1), ((0,), (0,)))
    for j in range(nd):
        gpart_ref[j] = gram[j * gram_rows : (j + 1) * gram_rows, :]
    started += exchange(
        "dp", d, nd, lambda j, p: gpart_ref.at[p], lambda j, p: gin_ref.at[j], s_gram, r_gram
    )
    pairs = nd // 2
    high, low = d // 2, d % 2
    mate = d + 1 - 2 * low
    cross = dot_bf16(responses, sketch, ((0,), (0,)))
    for j in range(nd):
        cpart_ref[j % 2, j // 2] = cross[j * cross_rows : (j + 1) * cross_rows, :]
    places = [lax.rem(high + j, pairs) for j in range(1, pairs)] + [high]

    for j, place in enumerate(places):
        started.append(
            send("dp", mate, cpart_ref.at[1 - low, place], cmate_ref.at[place], s_mate.at[j], r_mate.at[j])
        )
    arrived("dp", d, nd, lambda j, p: gin_ref.at[j], s_gram, r_gram)
    total = gpart_ref[d]
    for j in range(1, nd):
        total = total + gin_ref[j]
    gsum_ref[c, d] = total
    def add_mate(j):
        place = places[j]
        expect("dp", mate, cmate_ref.at[place], s_mate.at[j], r_mate.at[j])
        cmate_ref[place] = cmate_ref[place] + cpart_ref[low, place]

    started += gather_rows(
        d, nd, c, nc, lambda k, i: gsum_ref.at[k, i],
        (s_rows, r_rows), (s_rows2, r_rows2), (s_blocks, r_blocks), (s_blocks2, r_blocks2),
    )
    for first in range(nc):
        for k in range(half + 1):
            second = first + k
            lanes = slice(k * share, (k + 1) * share)
            if second < nc:
                for j in range(nd):
                    top = first * share + j * gram_rows
                    big_ref[top : top + gram_rows, second * share : (second + 1) * share] = gsum_ref[
                        first, j, :, lanes
                    ]
            elif k < half:
                for j in range(nd):
                    work_ref[j * gram_rows : (j + 1) * gram_rows, 0:share] = gsum_ref[first, j, :, lanes]
                second -= nc
                big_ref[
                    second * share : (second + 1) * share, first * share : (first + 1) * share
                ] = jnp.transpose(work_ref[0:share, 0:share])
    if share < BLOCK:
        full = big_ref[...]
        square = (size, size)
        above = lax.broadcasted_iota(jnp.int32, square, 1) > lax.broadcasted_iota(jnp.int32, square, 0)
        big_ref[...] = jnp.where(above, full, jnp.transpose(full))

    def pass_on(first, end):
        for j in range(first, end):
            add_mate(j)
            place = places[j]
            send(
                "dp", 2 * place + low, cmate_ref.at[place], cin_ref.at[j + 1],
                s_cross.at[j + 1], r_cross.at[j + 1],
            )

    pass_on(0, pairs - 1)
    eliminate(big_ref, work_ref, stack_ref, diag_ref, size)
    square = (size, size)
    row_of = lax.broadcasted_iota(jnp.int32, square, 0)
    lane_of = lax.broadcasted_iota(jnp.int32, square, 1)
    inverse = jnp.where(lane_of <= row_of, big_ref[...], 0.0)
    ih, im, il = split3(inverse)
    add_mate(pairs - 1)
    own = cmate_ref[high]
    for j in range(1, pairs):
        sender = 2 * lax.rem(high + pairs - j, pairs) + low
        expect("dp", sender, cin_ref.at[j], s_cross.at[j], r_cross.at[j])
        own = own + cin_ref[j]
    oh, om, ol = split3(own)
    inner = ((1,), (1,))
    coeffs = dot_bf16(oh, il, inner) + dot_bf16(om, im, inner) + dot_bf16(ol, ih, inner)
    coeffs = coeffs + dot_bf16(oh, im, inner) + dot_bf16(om, ih, inner)
    coeffs = (coeffs + dot_bf16(oh, ih, inner)).astype(BF16)
    outer = ((1,), (0,))
    mapped = dot_bf16(coeffs, il, outer) + dot_bf16(coeffs, im, outer)
    map_ref[d] = (mapped + dot_bf16(coeffs, ih, outer)).astype(BF16)
    started += gather("dp", d, nd, lambda i: map_ref.at[i], s_map, r_map, s_map2, r_map2)
    if last:
        scale = 1.0 / math.sqrt(total_rows)
        upper_ref[...] = jnp.where(lane_of >= row_of, big_ref[...], 0.0) * scale
        for b in range(size // BLOCK):
            at = slice(b * BLOCK, (b + 1) * BLOCK)
            upper_ref[at, at] = diag_ref[b] * scale
    for j in range(1, pairs):
        place = lax.rem(high + j, pairs)
        pltpu.make_async_remote_copy(
            src_ref=cmate_ref.at[place],
            dst_ref=cin_ref.at[j],
            send_sem=s_cross.at[j],
            recv_sem=r_cross.at[j],
            device_id={"dp": 2 * place + low},
            device_id_type=pl.DeviceIdType.MESH,
        ).wait_send()
    if cross_rows % 16 == 0:
        mapped = jnp.concatenate([map_ref[j] for j in range(nd)], axis=0)
    else:
        mapped = jnp.concatenate([map_ref[j].astype(F32) for j in range(nd)], axis=0).astype(BF16)
    restored = dot_bf16(sketch, mapped, ((1,), (1,)))
    if not last:
        restored = jnp.maximum(restored, 0.0)
    out_ref[...] = restored[0:rows, :].astype(BF16)
    for copy in started:
        copy.wait_send()


def first_kernel(nd, nc, total_rows, field_ref, weight_ref, probe_ref, out_ref, *rest):
    layer_kernel(nd, nc, False, total_rows, field_ref, weight_ref, probe_ref, out_ref, None, *rest)


def last_kernel(nd, nc, total_rows, *refs):
    layer_kernel(nd, nc, True, total_rows, *refs)


def layer(field, weight, probe, last):
    nd, nc = lax.axis_size("dp"), lax.axis_size("chan")
    rows, width = field.shape
    size = probe.shape[1]
    padded = -(-rows // 16) * 16
    share = size // nc
    gram_rows = share // nd
    gram_lanes = (nc // 2 + 1) * share
    cross_rows = width // nd
    restored = jax.ShapeDtypeStruct((rows, width), BF16)
    upper = jax.ShapeDtypeStruct((size, size), F32)
    chan_sems = pltpu.SemaphoreType.DMA((nc,))
    dp_sems = pltpu.SemaphoreType.DMA((nd,))
    return pl.pallas_call(
        functools.partial(last_kernel if last else first_kernel, nd, nc, rows * nd),
        out_shape=(restored, upper) if last else restored,
        in_specs=[pl.BlockSpec(memory_space=pl.ANY)] * 3,
        scratch_shapes=[
            pltpu.VMEM((rows + 2 * PAD, width), F32),
            pltpu.VMEM((padded, width), BF16),
            pltpu.VMEM((nc, padded, share), BF16),
            pltpu.VMEM((nc, padded, share), BF16),
            pltpu.VMEM((nc, padded, share), BF16),
            pltpu.VMEM((nd, gram_rows, gram_lanes), F32),
            pltpu.VMEM((nd, gram_rows, gram_lanes), F32),
            pltpu.VMEM((nc, nd, gram_rows, gram_lanes), F32),
            pltpu.VMEM((2, nd // 2, cross_rows, size), F32),
            pltpu.VMEM((nd // 2, cross_rows, size), F32),
            pltpu.VMEM((nd // 2, cross_rows, size), F32),
            pltpu.VMEM((nd, cross_rows, size), BF16),
            pltpu.VMEM((size, size), F32),
            pltpu.VMEM((BLOCK, 2 * BLOCK), F32),
            pltpu.VMEM((6 * BLOCK, size), BF16),
            pltpu.VMEM((size // BLOCK, BLOCK, BLOCK), F32),
        ]
        + [chan_sems] * 6
        + [dp_sems] * 14
        + [pltpu.SemaphoreType.DMA((nd, nc // 2))] * 4
        + [
            pltpu.SemaphoreType.DMA((3,)),
            pltpu.VMEM(field.shape, BF16),
            pltpu.VMEM(weight.shape, BF16),
            pltpu.VMEM(probe.shape, BF16),
        ],
        compiler_params=pltpu.CompilerParams(
            vmem_limit_bytes=VMEM_LIMIT, collective_id=1 if last else 0, has_side_effects=True
        ),
    )(field, weight, probe)


def per_device(inputs, conv_one, conv_two, probe_one, probe_two):
    activated = layer(inputs, conv_one, probe_one, False)
    return layer(activated, conv_two, probe_two, True)


def solution(mesh):
    in_specs = (
        P("dp", "chan"),
        P(None, None, "chan"),
        P(None, None, "chan"),
        P("chan", None),
        P("chan", None),
    )
    return jax.shard_map(
        per_device, mesh=mesh, in_specs=in_specs, out_specs=(P("dp", "chan"), P()), check_vma=False
    )
```

```python
import functools
import math

import jax
import jax.numpy as jnp
from jax import lax
from jax.experimental import pallas as pl
from jax.experimental.pallas import tpu as pltpu
from jax.sharding import PartitionSpec as P

SIDE = 7
PAD = 16
BLOCK = 128
PANEL = 16
F32 = jnp.float32
BF16 = jnp.bfloat16
VMEM_LIMIT = 48 * 1024 * 1024


def dot_f32(a, b, dims):
    return lax.dot_general(
        a, b, (dims, ((), ())), preferred_element_type=F32, precision=lax.Precision.HIGHEST
    )


def dot_bf16(a, b, dims):
    return lax.dot_general(a, b, (dims, ((), ())), preferred_element_type=F32)


def conv_into(field_ref, weight_ref, pad_ref, out_ref):
    rows, width = field_ref.shape
    group = weight_ref.shape[1]
    lanes = min(256, width)
    pad_ref[0:PAD, :] = jnp.zeros((PAD, width), F32)
    pad_ref[PAD + rows : PAD + rows + PAD, :] = jnp.zeros((PAD, width), F32)
    pad_ref[PAD : PAD + rows, :] = field_ref[...].astype(F32)
    place = lax.broadcasted_iota(jnp.int32, (rows, lanes), 0).astype(F32)
    pixel = place - (SIDE * SIDE) * jnp.floor((place + 0.5) * (1.0 / (SIDE * SIDE)))
    line = jnp.floor((pixel + 0.5) * (1.0 / SIDE))
    column = pixel - SIDE * line
    one, zero = jnp.ones((), F32), jnp.zeros((), F32)
    line_ok = (jnp.where(line > 0.5, one, zero), None, jnp.where(line < SIDE - 1.5, one, zero))
    column_ok = (jnp.where(column > 0.5, one, zero), None, jnp.where(column < SIDE - 1.5, one, zero))
    same = (
        lax.broadcasted_iota(jnp.int32, (lanes, lanes), 0) // group
        == lax.broadcasted_iota(jnp.int32, (lanes, lanes), 1) // group
    )
    for start in range(0, width, lanes):
        total = None
        for a in range(3):
            for b in range(3):
                shift = (a - 1) * SIDE + (b - 1)
                window = pad_ref[PAD + shift : PAD + shift + rows, start : start + lanes]
                if line_ok[a] is not None:
                    window = window * line_ok[a]
                if column_ok[b] is not None:
                    window = window * column_ok[b]
                small = weight_ref[3 * a + b, :, start : start + lanes]
                full = jnp.concatenate([small] * (lanes // group), axis=0)
                full = jnp.where(same, full, jnp.zeros((), BF16))
                part = dot_bf16(window.astype(BF16), full, ((1,), (0,)))
                total = part if total is None else total + part
        out_ref[0:rows, start : start + lanes] = total.astype(BF16)
    if out_ref.shape[0] > rows:
        out_ref[rows:, :] = jnp.zeros((out_ref.shape[0] - rows, width), BF16)


def split3(x):
    high = x.astype(BF16)
    rest = x - high.astype(F32)
    middle = rest.astype(BF16)
    low = (rest - middle.astype(F32)).astype(BF16)
    return high, middle, low


def stack_first(x, axis):
    h, m, l = split3(x)
    return jnp.concatenate([h, h, m, h, l, m], axis=axis)


def stack_second(x):
    h, m, l = split3(x)
    return jnp.concatenate([h, m, h, l, h, m], axis=0)


def eliminate_block(work_ref):
    row_of = lax.broadcasted_iota(jnp.int32, (PANEL, BLOCK), 0)
    for panel in range(BLOCK // PANEL):
        top = panel * PANEL
        left = work_ref[top : top + PANEL, 0:BLOCK]
        right = work_ref[top : top + PANEL, BLOCK : 2 * BLOCK]
        cols = [
            jnp.broadcast_to(left[:, top + k : top + k + 1], (PANEL, BLOCK)) for k in range(PANEL)
        ]
        rest = top + PANEL
        if rest < BLOCK:
            before = stack_first(work_ref[:, top:rest], 1)
        upper_left, upper_right = jnp.zeros_like(left), jnp.zeros_like(right)
        inverse_of = jnp.zeros_like(left)
        for i in range(PANEL):
            pivot = jnp.broadcast_to(cols[i][i : i + 1, :], (PANEL, BLOCK))
            root = lax.rsqrt(pivot)
            square = root * root
            here = row_of == i
            inverse_of = jnp.where(here, square, inverse_of)
            left_row, right_row = left[i : i + 1, :], right[i : i + 1, :]
            upper_left = jnp.where(here, left_row * root, upper_left)
            upper_right = jnp.where(here, right_row * root, upper_right)
            others = jnp.where(here, 0.0, cols[i])
            if i + 1 < PANEL:
                cols[i + 1] = cols[i + 1] - (others * cols[i + 1][i : i + 1, :]) * square
            factor = others * square
            for k in range(i + 2, PANEL):
                cols[k] = cols[k] - factor * cols[k][i : i + 1, :]
            left = left - factor * left_row
            right = right - factor * right_row
        lane_of = lax.broadcasted_iota(jnp.int32, (PANEL, BLOCK), 1)
        work_ref[top:rest, 0:BLOCK] = jnp.where(lane_of >= top + row_of, upper_left, 0.0)
        work_ref[top:rest, BLOCK : 2 * BLOCK] = upper_right
        if rest < BLOCK:
            second = jnp.concatenate(
                [stack_second(left * inverse_of), stack_second(right * inverse_of)], axis=1
            )
            update = dot_bf16(before, second, ((1,), (0,)))
            work_ref[rest:BLOCK, :] = work_ref[rest:BLOCK, :] - update[rest:BLOCK, :]


def eliminate(big_ref, work_ref, stack_ref, diag_ref, size, between):
    blocks = size // BLOCK
    square = (BLOCK, BLOCK)
    eye = jnp.where(
        lax.broadcasted_iota(jnp.int32, square, 0) == lax.broadcasted_iota(jnp.int32, square, 1),
        1.0,
        0.0,
    )

    @pl.loop(0, blocks)
    def _(b):
        for step, task in enumerate(between):
            pl.when(b == step + 1)(task)
        at = pl.ds(pl.multiple_of(b * BLOCK, BLOCK), BLOCK)
        work_ref[:, 0:BLOCK] = big_ref[at, at]
        work_ref[:, BLOCK : 2 * BLOCK] = eye
        eliminate_block(work_ref)
        diag_ref[b] = work_ref[:, 0:BLOCK]
        inverse = work_ref[:, BLOCK : 2 * BLOCK]
        big_ref[at, at] = eye
        row = dot_bf16(stack_first(inverse, 1), stack_second(big_ref[at, :]), ((1,), (0,)))
        big_ref[at, :] = row
        stack_ref[...] = stack_second(row)

        @pl.loop(b + 1, blocks)
        def _(other):
            to = pl.ds(pl.multiple_of(other * BLOCK, BLOCK), BLOCK)
            big_ref[to, at] = jnp.zeros(square, F32)
            factor = stack_first(big_ref[at, to], 0)
            big_ref[to, :] = big_ref[to, :] - dot_bf16(factor, stack_ref[...], ((0,), (0,)))


def exchange(axis, me, count, source, target, send_sem, recv_sem):
    copies = []
    for j in range(1, count):
        peer = lax.rem(me + j, count)
        copy = pltpu.make_async_remote_copy(
            src_ref=source(j, peer),
            dst_ref=target(j, peer),
            send_sem=send_sem.at[j],
            recv_sem=recv_sem.at[j],
            device_id={axis: peer},
            device_id_type=pl.DeviceIdType.MESH,
        )
        copy.start()
        copies.append(copy)
    return copies


def arrived(axis, me, count, target, send_sem, recv_sem):
    for j in range(1, count):
        sender = lax.rem(me + count - j, count)
        pltpu.make_async_remote_copy(
            src_ref=target(j, sender),
            dst_ref=target(j, sender),
            send_sem=send_sem.at[j],
            recv_sem=recv_sem.at[j],
            device_id={axis: sender},
            device_id_type=pl.DeviceIdType.MESH,
        ).wait_recv()


def send(axis, peer, source, target, send_sem, recv_sem):
    copy = pltpu.make_async_remote_copy(
        src_ref=source,
        dst_ref=target,
        send_sem=send_sem,
        recv_sem=recv_sem,
        device_id={axis: peer},
        device_id_type=pl.DeviceIdType.MESH,
    )
    copy.start()
    return copy


def expect(axis, sender, target, send_sem, recv_sem):
    pltpu.make_async_remote_copy(
        src_ref=target,
        dst_ref=target,
        send_sem=send_sem,
        recv_sem=recv_sem,
        device_id={axis: sender},
        device_id_type=pl.DeviceIdType.MESH,
    ).wait_recv()


def gather(axis, me, count, slot, far_send, far_recv, mate_send, mate_recv):
    high, low = me // 2, me % 2
    mate = me + 1 - 2 * low
    pairs = count // 2
    copies = [
        send(axis, 2 * lax.rem(high + j, pairs) + low, slot(me), slot(me), far_send.at[j], far_recv.at[j])
        for j in range(1, pairs)
    ]
    copies.append(send(axis, mate, slot(me), slot(me), mate_send.at[0], mate_recv.at[0]))
    for j in range(1, pairs):
        sender = 2 * lax.rem(high + pairs - j, pairs) + low
        expect(axis, sender, slot(sender), far_send.at[j], far_recv.at[j])
        copies.append(send(axis, mate, slot(sender), slot(sender), mate_send.at[j], mate_recv.at[j]))
    expect(axis, mate, slot(mate), mate_send.at[0], mate_recv.at[0])
    for j in range(1, pairs):
        origin = 2 * lax.rem(high + pairs - j, pairs) + 1 - low
        expect(axis, mate, slot(origin), mate_send.at[j], mate_recv.at[j])
    return copies


def gather_rows(d, nd, c, nc, slot, far, mate_sems, chan_far, chan_mate, middle):
    high, low = d // 2, d % 2
    mate = d + 1 - 2 * low
    pairs = nd // 2
    chan_high, chan_low = c // 2, c % 2
    chan_other = c + 1 - 2 * chan_low
    chan_pairs = nc // 2
    copies = []

    def over_chan(order, piece):
        ref = slot(c, piece)
        for j in range(1, chan_pairs):
            peer = 2 * lax.rem(chan_high + j, chan_pairs) + chan_low
            copies.append(send("chan", peer, ref, ref, chan_far[0].at[order, j], chan_far[1].at[order, j]))
        copies.append(send("chan", chan_other, ref, ref, chan_mate[0].at[order, 0], chan_mate[1].at[order, 0]))

    mine = slot(c, d)
    for j in range(1, pairs):
        peer = 2 * lax.rem(high + j, pairs) + low
        copies.append(send("dp", peer, mine, mine, far[0].at[j], far[1].at[j]))
    copies.append(send("dp", mate, mine, mine, mate_sems[0].at[0], mate_sems[1].at[0]))
    over_chan(0, d)
    pieces = [d, mate]
    expect("dp", mate, slot(c, mate), mate_sems[0].at[0], mate_sems[1].at[0])
    over_chan(1, mate)
    for j in range(1, pairs):
        sender = 2 * lax.rem(high + pairs - j, pairs) + low
        piece = slot(c, sender)
        expect("dp", sender, piece, far[0].at[j], far[1].at[j])
        copies.append(send("dp", mate, piece, piece, mate_sems[0].at[j], mate_sems[1].at[j]))
        over_chan(2 * j, sender)
        pieces.append(sender)
        origin = 2 * lax.rem(high + pairs - j, pairs) + 1 - low
        expect("dp", mate, slot(c, origin), mate_sems[0].at[j], mate_sems[1].at[j])
        over_chan(2 * j + 1, origin)
        pieces.append(origin)
    middle()
    for order, piece in enumerate(pieces):
        for j in range(1, chan_pairs):
            sender = 2 * lax.rem(chan_high + chan_pairs - j, chan_pairs) + chan_low
            ref = slot(sender, piece)
            expect("chan", sender, ref, chan_far[0].at[order, j], chan_far[1].at[order, j])
            copies.append(
                send("chan", chan_other, ref, ref, chan_mate[0].at[order, j], chan_mate[1].at[order, j])
            )
    for order, piece in enumerate(pieces):
        for j in range(chan_pairs):
            origin = 2 * lax.rem(chan_high + chan_pairs - j, chan_pairs) + 1 - chan_low
            expect(
                "chan", chan_other, slot(origin, piece), chan_mate[0].at[order, j], chan_mate[1].at[order, j]
            )
    return copies


def layer_kernel(
    nd, nc, last, total_rows,
    field_any, weight_any, probe_any, out_ref, upper_ref,
    pad_ref, resp_ref, part_ref, part_in_ref, sketch_ref, gpart_ref, gin_ref, gsum_ref,
    cpart_ref, cmate_ref, cin_ref, map_ref, big_ref, work_ref, stack_ref, diag_ref,
    s_part, r_part, s_sketch, r_sketch, s_sketch2, r_sketch2,
    s_gram, r_gram, s_rows, r_rows, s_rows2, r_rows2, s_mate, r_mate, s_cross, r_cross,
    s_map, r_map, s_map2, r_map2, s_blocks, r_blocks, s_blocks2, r_blocks2, s_load,
    field_ref, weight_ref, probe_ref,
):
    loads = [
        pltpu.make_async_copy(source, target, s_load.at[k])
        for k, (source, target) in enumerate(
            ((field_any, field_ref), (weight_any, weight_ref), (probe_any, probe_ref))
        )
    ]
    for load in loads:
        load.start()
    d = lax.axis_index("dp")
    c = lax.axis_index("chan")
    rows, width = field_ref.shape
    size = probe_ref.shape[1]
    padded = resp_ref.shape[0]
    share = size // nc
    gram_rows = share // nd
    cross_rows = width // nd

    barrier = pltpu.get_barrier_semaphore()
    for j in range(1, nd):
        pl.semaphore_signal(
            barrier, inc=1, device_id={"dp": lax.rem(d + j, nd)}, device_id_type=pl.DeviceIdType.MESH
        )
    for j in range(1, nc):
        pl.semaphore_signal(
            barrier, inc=1, device_id={"chan": lax.rem(c + j, nc)}, device_id_type=pl.DeviceIdType.MESH
        )

    big_ref[...] = jnp.zeros((size, size), F32)
    loads[0].wait()
    loads[1].wait()
    conv_into(field_ref, weight_ref, pad_ref, resp_ref)
    responses = resp_ref[...]
    loads[2].wait()
    for j in range(nc):
        block = dot_bf16(responses, probe_ref[:, j * share : (j + 1) * share], ((1,), (0,)))
        part_ref[j] = block.astype(BF16)
    pl.semaphore_wait(barrier, nd + nc - 2)

    started = exchange(
        "chan", c, nc, lambda j, p: part_ref.at[p], lambda j, p: part_in_ref.at[j], s_part, r_part
    )
    arrived("chan", c, nc, lambda j, p: part_in_ref.at[j], s_part, r_part)
    mine = part_ref[c].astype(F32)
    for j in range(1, nc):
        mine = mine + part_in_ref[j].astype(F32)
    mine = mine.astype(BF16)
    sketch_ref[c] = mine
    started += gather(
        "chan", c, nc, lambda i: sketch_ref.at[i], s_sketch, r_sketch, s_sketch2, r_sketch2
    )
    sketch = jnp.concatenate([sketch_ref[j] for j in range(nc)], axis=1)

    half = nc // 2
    ahead = [mine] + [sketch_ref[lax.rem(c + k, nc)] for k in range(1, half + 1)]
    gram = dot_bf16(mine, jnp.concatenate(ahead, axis=1), ((0,), (0,)))
    for j in range(nd):
        gpart_ref[j] = gram[j * gram_rows : (j + 1) * gram_rows, :]
    started += exchange(
        "dp", d, nd, lambda j, p: gpart_ref.at[p], lambda j, p: gin_ref.at[j], s_gram, r_gram
    )
    pairs = nd // 2
    high, low = d // 2, d % 2
    mate = d + 1 - 2 * low
    cross = dot_bf16(responses, sketch, ((0,), (0,)))
    for j in range(nd):
        cpart_ref[j % 2, j // 2] = cross[j * cross_rows : (j + 1) * cross_rows, :]
    arrived("dp", d, nd, lambda j, p: gin_ref.at[j], s_gram, r_gram)
    total = gpart_ref[d]
    for j in range(1, nd):
        total = total + gin_ref[j]
    gsum_ref[c, d] = total
    places = [lax.rem(high + j, pairs) for j in range(1, pairs)] + [high]

    def middle():
        for j, place in enumerate(places):
            started.append(
                send("dp", mate, cpart_ref.at[1 - low, place], cmate_ref.at[place], s_mate.at[j], r_mate.at[j])
            )

    def add_mate(j):
        place = places[j]
        expect("dp", mate, cmate_ref.at[place], s_mate.at[j], r_mate.at[j])
        cmate_ref[place] = cmate_ref[place] + cpart_ref[low, place]

    started += gather_rows(
        d, nd, c, nc, lambda k, i: gsum_ref.at[k, i],
        (s_rows, r_rows), (s_rows2, r_rows2), (s_blocks, r_blocks), (s_blocks2, r_blocks2), middle,
    )
    for first in range(nc):
        for k in range(half + 1):
            second = first + k
            lanes = slice(k * share, (k + 1) * share)
            if second < nc:
                for j in range(nd):
                    top = first * share + j * gram_rows
                    big_ref[top : top + gram_rows, second * share : (second + 1) * share] = gsum_ref[
                        first, j, :, lanes
                    ]
            elif k < half:
                for j in range(nd):
                    work_ref[j * gram_rows : (j + 1) * gram_rows, 0:share] = gsum_ref[first, j, :, lanes]
                second -= nc
                big_ref[
                    second * share : (second + 1) * share, first * share : (first + 1) * share
                ] = jnp.transpose(work_ref[0:share, 0:share])
    if share < BLOCK:
        full = big_ref[...]
        square = (size, size)
        above = lax.broadcasted_iota(jnp.int32, square, 1) > lax.broadcasted_iota(jnp.int32, square, 0)
        big_ref[...] = jnp.where(above, full, jnp.transpose(full))

    def pass_on(first, end):
        for j in range(first, end):
            add_mate(j)
            place = places[j]
            send(
                "dp", 2 * place + low, cmate_ref.at[place], cin_ref.at[j + 1],
                s_cross.at[j + 1], r_cross.at[j + 1],
            )

    early = pairs // 2
    between = (lambda: pass_on(0, early), lambda: pass_on(early, pairs - 1))
    eliminate(big_ref, work_ref, stack_ref, diag_ref, size, between)
    square = (size, size)
    row_of = lax.broadcasted_iota(jnp.int32, square, 0)
    lane_of = lax.broadcasted_iota(jnp.int32, square, 1)
    inverse = jnp.where(lane_of <= row_of, big_ref[...], 0.0)
    ih, im, il = split3(inverse)
    add_mate(pairs - 1)
    own = cmate_ref[high]
    for j in range(1, pairs):
        sender = 2 * lax.rem(high + pairs - j, pairs) + low
        expect("dp", sender, cin_ref.at[j], s_cross.at[j], r_cross.at[j])
        own = own + cin_ref[j]
    oh, om, ol = split3(own)
    inner = ((1,), (1,))
    coeffs = dot_bf16(oh, il, inner) + dot_bf16(om, im, inner) + dot_bf16(ol, ih, inner)
    coeffs = coeffs + dot_bf16(oh, im, inner) + dot_bf16(om, ih, inner)
    coeffs = (coeffs + dot_bf16(oh, ih, inner)).astype(BF16)
    outer = ((1,), (0,))
    mapped = dot_bf16(coeffs, il, outer) + dot_bf16(coeffs, im, outer)
    map_ref[d] = (mapped + dot_bf16(coeffs, ih, outer)).astype(BF16)
    started += gather("dp", d, nd, lambda i: map_ref.at[i], s_map, r_map, s_map2, r_map2)
    if last:
        scale = 1.0 / math.sqrt(total_rows)
        upper_ref[...] = jnp.where(lane_of >= row_of, big_ref[...], 0.0) * scale
        for b in range(size // BLOCK):
            at = slice(b * BLOCK, (b + 1) * BLOCK)
            upper_ref[at, at] = diag_ref[b] * scale
    for j in range(1, pairs):
        place = lax.rem(high + j, pairs)
        pltpu.make_async_remote_copy(
            src_ref=cmate_ref.at[place],
            dst_ref=cin_ref.at[j],
            send_sem=s_cross.at[j],
            recv_sem=r_cross.at[j],
            device_id={"dp": 2 * place + low},
            device_id_type=pl.DeviceIdType.MESH,
        ).wait_send()
    if cross_rows % 16 == 0:
        mapped = jnp.concatenate([map_ref[j] for j in range(nd)], axis=0)
    else:
        mapped = jnp.concatenate([map_ref[j].astype(F32) for j in range(nd)], axis=0).astype(BF16)
    restored = dot_bf16(sketch, mapped, ((1,), (1,)))
    if not last:
        restored = jnp.maximum(restored, 0.0)
    out_ref[...] = restored[0:rows, :].astype(BF16)
    for copy in started:
        copy.wait_send()


def first_kernel(nd, nc, total_rows, field_ref, weight_ref, probe_ref, out_ref, *rest):
    layer_kernel(nd, nc, False, total_rows, field_ref, weight_ref, probe_ref, out_ref, None, *rest)


def last_kernel(nd, nc, total_rows, *refs):
    layer_kernel(nd, nc, True, total_rows, *refs)


def layer(field, weight, probe, last):
    nd, nc = lax.axis_size("dp"), lax.axis_size("chan")
    rows, width = field.shape
    size = probe.shape[1]
    padded = -(-rows // 16) * 16
    share = size // nc
    gram_rows = share // nd
    gram_lanes = (nc // 2 + 1) * share
    cross_rows = width // nd
    restored = jax.ShapeDtypeStruct((rows, width), BF16)
    upper = jax.ShapeDtypeStruct((size, size), F32)
    chan_sems = pltpu.SemaphoreType.DMA((nc,))
    dp_sems = pltpu.SemaphoreType.DMA((nd,))
    return pl.pallas_call(
        functools.partial(last_kernel if last else first_kernel, nd, nc, rows * nd),
        out_shape=(restored, upper) if last else restored,
        in_specs=[pl.BlockSpec(memory_space=pl.ANY)] * 3,
        scratch_shapes=[
            pltpu.VMEM((rows + 2 * PAD, width), F32),
            pltpu.VMEM((padded, width), BF16),
            pltpu.VMEM((nc, padded, share), BF16),
            pltpu.VMEM((nc, padded, share), BF16),
            pltpu.VMEM((nc, padded, share), BF16),
            pltpu.VMEM((nd, gram_rows, gram_lanes), F32),
            pltpu.VMEM((nd, gram_rows, gram_lanes), F32),
            pltpu.VMEM((nc, nd, gram_rows, gram_lanes), F32),
            pltpu.VMEM((2, nd // 2, cross_rows, size), F32),
            pltpu.VMEM((nd // 2, cross_rows, size), F32),
            pltpu.VMEM((nd // 2, cross_rows, size), F32),
            pltpu.VMEM((nd, cross_rows, size), BF16),
            pltpu.VMEM((size, size), F32),
            pltpu.VMEM((BLOCK, 2 * BLOCK), F32),
            pltpu.VMEM((6 * BLOCK, size), BF16),
            pltpu.VMEM((size // BLOCK, BLOCK, BLOCK), F32),
        ]
        + [chan_sems] * 6
        + [dp_sems] * 14
        + [pltpu.SemaphoreType.DMA((nd, nc // 2))] * 4
        + [
            pltpu.SemaphoreType.DMA((3,)),
            pltpu.VMEM(field.shape, BF16),
            pltpu.VMEM(weight.shape, BF16),
            pltpu.VMEM(probe.shape, BF16),
        ],
        compiler_params=pltpu.CompilerParams(
            vmem_limit_bytes=VMEM_LIMIT, collective_id=1 if last else 0, has_side_effects=True
        ),
    )(field, weight, probe)


def per_device(inputs, conv_one, conv_two, probe_one, probe_two):
    activated = layer(inputs, conv_one, probe_one, False)
    return layer(activated, conv_two, probe_two, True)


def solution(mesh):
    in_specs = (
        P("dp", "chan"),
        P(None, None, "chan"),
        P(None, None, "chan"),
        P("chan", None),
        P("chan", None),
    )
    return jax.shard_map(
        per_device, mesh=mesh, in_specs=in_specs, out_specs=(P("dp", "chan"), P()), check_vma=False
    )
```
